32 devices in a mesh: comp: 4 (over z), tile: 8 (over y, x, core).
Axes of the slice: x: 2, y: 2, z: 4, core: 2. Of those that a mesh axis runs over, the one named last changes fastest.
Arguments:
- atmos_state: float32 [4, 32, 32, 1024], P(None, None, 'comp', 'tile'), may hold values from -6 to 6
- ocean_state: float32 [4, 8, 64, 1024], P(None, None, 'comp', 'tile'), may hold values from -6 to 6
- flux_coef: float32 [4], replicated, may hold values from 0.5 to 2
- remap_weight: bfloat16 [384, 128, 128], P(('comp', 'tile')), may hold values from -0.5 to 0.5
- source_row: int32 [384], P(('comp', 'tile')), may hold values from 0 to 7
- target_device: int32 [384, 1], P(('comp', 'tile')), may hold values from 0 to 7; in each aligned block of 12 rows (0 to 11, 12 to 23, ...) at most 3 rows name the same one
- target_row: int32 [384], P(('comp', 'tile')), may hold values from 0 to 15
Outputs:
- atmos_next: float32 [4, 32, 32, 1024], P(None, None, 'comp', 'tile')
- ocean_next: float32 [4, 8, 64, 1024], P(None, None, 'comp', 'tile')
The draws below stay inside these ranges and needn't reach their ends.
Inputs may be any that keep to these rules, and one draw needn't show every extreme that they name: `target_device`: among the items of one device no target device is named more than 3 times, and some target device is named exactly 3 times.
All inputs are finite; a program needn't handle non-finite values.
Results may differ from the reference program's by a relative error of at most 0.0024.
Values sent between devices are 32-bit elements; how exact they have to be, the bound alone decides.
No kernel may reach another device: no remote copies, remote signals or barrier semaphores. Data moves between devices by JAX's collectives and lax.ppermute only.
A program may use at most 64 MiB of HBM per device.

```python
import math
import jax
import jax.numpy as jnp
import numpy as np
from jax import lax

FIELDS = 4
TW = 128
ALEV = 32
AY = 8
OLEV = 8
OY = 16
CAP = 3
ITEMS_DEV = 12
ITEMS = 384
NYA = 32
NXA = 1024
NYO = 64
NXO = 1024
N_COMP = 4
N_TILE = 8


def touch_ends(values, stream_key, low, largest):
    shape = values.shape
    spot = [jax.random.randint(jax.random.fold_in(stream_key, axis), (), 0, shape[axis]) for axis in range(len(shape))]
    values = values.at[tuple(spot)].set(low)
    longest = shape.index(max(shape))
    spot[longest] = (spot[longest] + 1) % shape[longest]
    return values.at[tuple(spot)].set(largest)


def levels(rng, dims, split, low, high):
    loudness = 1.0
    for dim, parts in split:
        draws = jax.random.uniform(jax.random.fold_in(jax.random.fold_in(rng, 6), dim), (parts,), jnp.float32, low / len(split), high / len(split))
        loudness = loudness * jnp.repeat(jnp.exp(draws), dims[dim] // parts).reshape((-1,) + (1,) * (len(dims) - 1 - dim))
    return loudness


def routed_block(own_key, own, number, rows, count, top, most, slope):
    sequence = jax.random.permutation(own_key, count)
    packed, common = portions_of(count, rows * top, most, slope, True), portions_of(count, rows * top, most, slope, False)
    places = jnp.arange(count)

    def named(sizes, offset_by):
        used = int((sizes > 0).sum())
        fixed = max(1, used // 4)
        moved = fixed + (places - fixed + offset_by * (used - fixed)) % max(1, count - fixed)
        return jnp.zeros((count,), jnp.int32).at[sequence[jnp.where(places < fixed, places, moved)]].set(jnp.asarray(sizes, jnp.int32))

    sizes = jnp.where(number % 4 == 0, named(packed, number // 4), named(common, number - number // 4 - 1))
    mixed = jax.random.permutation(jax.random.fold_in(own, 3), count)
    giver, receiver = mixed[0:count // 2 * 2:2], mixed[1:count // 2 * 2:2]
    slack = jnp.minimum(sizes[giver] - 1, most - sizes[receiver]) // 2
    slack = jnp.where((giver == sequence[0]) | (receiver == sequence[0]) | (sizes[receiver] == 0), 0, jnp.maximum(slack, 0))
    moved = jax.random.randint(jax.random.fold_in(own, 4), (count // 2,), 0, 1 << 20) % (slack + 1)
    sizes = sizes.at[giver].add(-moved).at[receiver].add(moved)
    labels = jnp.searchsorted(jnp.cumsum(sizes), jnp.arange(rows * top), side="right").astype(jnp.int32)
    listing = labels.reshape(top, rows).T
    listing = listing[jax.random.permutation(jax.random.fold_in(own, 1), rows)]
    offset_by = jax.random.randint(jax.random.fold_in(own, 2), (rows, 1), 0, top)
    return jnp.take_along_axis(listing, (jnp.arange(top)[None, :] + offset_by) % top, axis=1)


def portions_of(number_of, total, most, lean, full):
    portions = [(1 << 20) // math.isqrt(rank ** lean) + 1 for rank in range(1, number_of + 1)]
    largest = most if full else min(most, max(-(-total // number_of), total * portions[0] // sum(portions)))
    least = 1 if total - largest >= number_of - 1 else 0
    holding, rest = [largest] + [least] * (number_of - 1), total - largest - least * (number_of - 1)
    while rest > 0:
        movable = [i for i in range(1, number_of) if holding[i] < largest] or [i for i in range(1, number_of) if holding[i] < most]
        whole, remaining = sum([portions[i] for i in movable]), rest
        for i in movable:
            more = min(most - holding[i], max(1, remaining * portions[i] // whole), rest)
            holding[i] = holding[i] + more
            rest = rest - more
    return np.array(holding)


def centred(key, shape, spread, bound, cuts=(), held_as=jnp.bfloat16):
    level = levels(key, shape, cuts, -0.22, 0.18) if cuts else 1.0
    result = jax.random.normal(key, shape, jnp.float32) * spread * level
    return jnp.minimum(jnp.maximum(result, -bound), bound).astype(held_as)


def setup_inputs(seed: int = 0) -> dict:
    key_list = jax.random.split(jax.random.key(seed), 8)
    atmos_state = centred(key_list[0], (FIELDS, ALEV, NYA, NXA), 1.0, 6.0, ((2, 4), (3, 8)), jnp.float32)
    ocean_state = centred(key_list[1], (FIELDS, OLEV, NYO, NXO), 1.0, 6.0, ((2, 4), (3, 8)), jnp.float32)
    flux_coef = jnp.clip(jnp.exp(jax.random.uniform(key_list[2], (FIELDS,), jnp.float32, math.log(0.5), math.log(2.0))), 0.5, 2.0)
    remap_weight = centred(key_list[3], (ITEMS, TW, TW), TW ** -0.5, 0.5, ((0, 32),))
    source_row = touch_ends(jax.random.randint(key_list[4], (ITEMS,), 0, AY), jax.random.fold_in(key_list[4], 1), 0, AY - 1).astype(jnp.int32)
    target_device_keys = jax.random.split(jax.random.fold_in(key_list[5], 1), ITEMS // ITEMS_DEV)
    target_device_turns = jax.random.permutation(jax.random.fold_in(key_list[5], 3), ITEMS // ITEMS_DEV)
    target_device = jax.vmap(lambda own, number: routed_block(jax.random.fold_in(key_list[5], 2), own, number, ITEMS_DEV, N_TILE, 1, CAP, 2))(target_device_keys, target_device_turns).reshape((ITEMS, 1))
    target_row = touch_ends(jax.random.randint(key_list[6], (ITEMS,), 0, OY), jax.random.fold_in(key_list[6], 1), 0, OY - 1).astype(jnp.int32)
    return {"atmos_state": atmos_state, "ocean_state": ocean_state, "flux_coef": flux_coef, "remap_weight": remap_weight, "source_row": source_row, "target_device": target_device, "target_row": target_row}


viscosity = 0.01
diffusion = 0.2
mixing_rate = 0.1
forcing_step = 0.5


def gll_second():
    nodes = [-1.0, -(0.2 ** 0.5), 0.2 ** 0.5, 1.0]
    derivative = []
    for outer_pos in range(4):
        entries = []
        for inner_pos in range(4):
            if outer_pos == inner_pos:
                value = sum(1.0 / (nodes[outer_pos] - nodes[other]) for other in range(4) if other != outer_pos)
            else:
                numerator = 1.0
                for other in range(4):
                    if other != outer_pos and other != inner_pos:
                        numerator = numerator * (nodes[outer_pos] - nodes[other])
                denominator = 1.0
                for other in range(4):
                    if other != inner_pos:
                        denominator = denominator * (nodes[inner_pos] - nodes[other])
                value = numerator / denominator
            entries.append(value)
        derivative.append(entries)
    squared = []
    for outer_pos in range(4):
        squared.append([sum(derivative[outer_pos][middle] * derivative[middle][inner_pos] for middle in range(4)) for inner_pos in range(4)])
    return squared


def seam_average(values, axis):
    position = lax.broadcasted_iota(jnp.int32, values.shape, axis) % 4
    after = jnp.roll(values, -1, axis)
    before = jnp.roll(values, 1, axis)
    return jnp.where(position == 3, (values + after) * 0.5, jnp.where(position == 0, (values + before) * 0.5, values))


def reference(atmos_state, ocean_state, flux_coef, remap_weight, source_row, target_device, target_row):
    highest = lax.Precision.HIGHEST
    second = jnp.array(gll_second(), jnp.float32)
    along_x = atmos_state.reshape(FIELDS, ALEV, NYA, NXA // 4, 4)
    second_x = jnp.einsum('flyek,ik->flyei', along_x, second, precision=highest).reshape(FIELDS, ALEV, NYA, NXA)
    along_y = atmos_state.reshape(FIELDS, ALEV, NYA // 4, 4, NXA)
    second_y = jnp.einsum('flekx,ik->fleix', along_y, second, precision=highest).reshape(FIELDS, ALEV, NYA, NXA)
    laplace = second_x + second_y
    smoothed = seam_average(seam_average(laplace, 3), 2)
    atmos_next = atmos_state + viscosity * smoothed

    surface = (flux_coef[:, None, None] * atmos_state[:, 0]).astype(jnp.bfloat16)
    tiles = surface.reshape(FIELDS, NYA, N_TILE, TW).transpose(1, 2, 0, 3).reshape(NYA * N_TILE, FIELDS, TW)
    device_count = N_COMP * N_TILE
    weights_by = remap_weight.reshape(device_count, ITEMS_DEV, TW, TW)
    sources_by = source_row.reshape(device_count, ITEMS_DEV).astype(jnp.int32)
    targets_by = target_device.reshape(device_count, ITEMS_DEV).astype(jnp.int32)
    rows_by = target_row.reshape(device_count, ITEMS_DEV).astype(jnp.int32)
    device_ids = jnp.arange(device_count, dtype=jnp.int32)

    def one_device(running_sum, inputs):
        device_id, weights, sources, targets, rows_to = inputs
        band = device_id // N_TILE
        column = device_id % N_TILE
        source_ids = ((band * AY + sources) * N_TILE + column).astype(jnp.int32)
        picked = tiles[source_ids].astype(jnp.float32)
        shares = jnp.einsum('ifk,ikj->ifj', picked, weights.astype(jnp.float32), precision=highest)
        target_ids = ((band * OY + rows_to) * N_TILE + targets).astype(jnp.int32)
        return running_sum.at[target_ids].add(shares), None

    start_sum = jnp.zeros((NYO * N_TILE, FIELDS, TW), jnp.float32)
    summed, unused = lax.scan(one_device, start_sum, (device_ids, weights_by, sources_by, targets_by, rows_by))
    remapped = summed.reshape(NYO, N_TILE, FIELDS, TW).transpose(2, 0, 1, 3).reshape(FIELDS, NYO, NXO)

    padded = jnp.pad(ocean_state, ((0, 0), (0, 0), (1, 1), (1, 1)))
    planar = padded[:, :, 2:, 1:-1] + padded[:, :, :-2, 1:-1] + padded[:, :, 1:-1, 2:] + padded[:, :, 1:-1, :-2] - 4.0 * ocean_state
    upper = jnp.concatenate([ocean_state[:, :1], ocean_state[:, :-1]], axis=1)
    lower = jnp.concatenate([ocean_state[:, 1:], ocean_state[:, -1:]], axis=1)
    vertical = upper + lower - 2.0 * ocean_state
    ocean_next = ocean_state + diffusion * planar + mixing_rate * vertical
    ocean_next = ocean_next.at[:, 0].add(forcing_step * remapped)
    return atmos_next, ocean_next
```

```python
import functools

import jax
import jax.numpy as jnp
import numpy as np
from jax import lax
from jax.experimental import pallas as pl
from jax.experimental.pallas import tpu as pltpu
from jax.sharding import PartitionSpec as P

viscosity = 0.01
diffusion = 0.2
mixing_rate = 0.1
forcing_step = 0.5
SLOTS = 3
GROUP = 4
BLOCK = (SLOTS + 1) * GROUP
HALO = 16


def gll_second():
    nodes = np.array([-1.0, -(0.2**0.5), 0.2**0.5, 1.0])
    derivative = np.zeros((4, 4))
    for i in range(4):
        for j in range(4):
            if i == j:
                derivative[i, j] = sum(1.0 / (nodes[i] - nodes[k]) for k in range(4) if k != i)
            else:
                top = np.prod([nodes[i] - nodes[k] for k in range(4) if k not in (i, j)])
                derivative[i, j] = top / np.prod([nodes[j] - nodes[k] for k in range(4) if k != j])
    return derivative @ derivative


def tables(columns):
    second = gll_second()
    along = np.kron(np.eye(columns // 4), second)
    seam = np.eye(columns)
    for x in range(0, columns, 4):
        for edge, other in ((x, x - 1), (x + 3, x + 4)):
            seam[edge, edge] = 0.5
            if 0 <= other < columns:
                seam[edge, other] = 0.5
    inner = (seam @ along).T
    first, last = np.eye(columns)[0], np.eye(columns)[-1]
    edge_atmos = np.zeros((16, 8 * columns))
    for k in range(8):
        for side, unit, row in ((0, first, along[0]), (8, last, along[-1])):
            edge_atmos[side + k, k * columns : (k + 1) * columns] += row
            for j in range(4):
                m = k // 4 * 4 + j
                edge_atmos[side + k, m * columns : (m + 1) * columns] += second[k % 4, j] * unit
    edge_ocean = np.zeros((16, 4 * columns))
    place_atmos = np.zeros((8, 16, columns))
    place_ocean = np.zeros((4, 16, columns))
    for c in range(4):
        edge_ocean[c, c * columns : (c + 1) * columns] = first
        edge_ocean[4 + c, c * columns : (c + 1) * columns] = last
        for part in (0, 8):
            place_ocean[c, part + c] = last
            place_ocean[c, part + 4 + c] = first
    for k in range(8):
        place_atmos[k, k] = 0.5 * first
        place_atmos[k, 8 + k] = 0.5 * last
    bf = lambda a: jnp.asarray(a.astype(np.float32)).astype(jnp.bfloat16)
    return (
        bf(np.concatenate([inner, seam.T])),
        bf(np.concatenate([edge_atmos, edge_ocean], axis=1)),
        bf(np.concatenate([place_atmos.reshape(-1, columns), place_ocean.reshape(-1, columns)])),
    )


def dot(a, b):
    return jnp.dot(a, b, preferred_element_type=jnp.float32)


def dot_nt(a, b):
    return lax.dot_general(a, b, (((1,), (1,)), ((), ())), preferred_element_type=jnp.float32)


def dot_tn(a, b):
    return lax.dot_general(a, b, (((0,), (0,)), ((), ())), preferred_element_type=jnp.float32)


def split(v):
    high = v.astype(jnp.bfloat16)
    return high, (v - high.astype(jnp.float32)).astype(jnp.bfloat16)


def row_of(ref, k, count, stride):
    return ref[pl.ds(k, count, stride=stride), :]


def along_y(rows, k):
    second = gll_second()
    base = k // 4 * 4
    return sum(float(second[k % 4, j]) * rows[base + j] for j in range(4))


def pack_kernel(
    n, fields, levels, olev, oy,
    coef, source, target, target_row, atmos, ocean, weight, mix, edge,
    blocks, far, edges, surf, counts,
):
    planes, cells = fields * levels, fields * olev
    ay = atmos.shape[0] // planes
    columns = atmos.shape[1]
    items = weight.shape[0]
    me = lax.axis_index("tile")
    even = me % 2 == 0
    rows = [row_of(atmos, k, planes, ay) for k in range(ay)]
    halves = [r.astype(jnp.bfloat16) for r in rows]
    inner, seam = mix[:columns, :], mix[columns:, :]
    for slot, k in ((0, 0), (1, ay - 1)):
        edges[slot, :planes, :] = dot(halves[k], inner) + dot(along_y(rows, k).astype(jnp.bfloat16), seam)
    cell_rows = [row_of(ocean, y, cells, oy) for y in range(oy)]
    edges[0, planes:, :] = cell_rows[0]
    edges[1, planes:, :] = cell_rows[oy - 1]
    width = ay * columns
    atmos_cols = dot_nt(edge[:, :width], jnp.concatenate(halves, axis=1))
    chunks = [jnp.concatenate(cell_rows[4 * c : 4 * c + 4], axis=0) for c in range(oy // 4)]
    parts = [split(c) for c in chunks]
    ocean_cols = dot_nt(edge[:, width:], jnp.concatenate([p[0] for p in parts], axis=1)) + dot_nt(
        edge[:, width:], jnp.concatenate([p[1] for p in parts], axis=1)
    )
    left, right = atmos_cols[:ay], atmos_cols[ay:]
    near = jnp.where(even, right, left)
    far[:ay, :] = jnp.where(even, left, right)
    far[ay:, :] = ocean_cols[:8]
    base = n * (SLOTS + 1)
    for g in range(2):
        blocks[base + g] = near[g * GROUP : (g + 1) * GROUP]
        blocks[base + 2 + g] = ocean_cols[g * GROUP : (g + 1) * GROUP]
    blocks[:base] = jnp.full((base, GROUP, columns), -1.0, jnp.float32)
    for y in range(ay):
        surf[y, fields:, :] = jnp.zeros((8 - fields, columns), jnp.float32)
    for f in range(fields):
        plane = atmos[f * levels * ay : f * levels * ay + ay, :] * coef[f]
        for y in range(ay):
            surf[y, f : f + 1, :] = plane[y : y + 1]

    @pl.loop(0, n)
    def _(i):
        counts[i] = 0

    def one(i, carry):
        to = target[i]
        slot = counts[to]
        counts[to] = slot + 1
        offset = to ^ me
        at = ((offset % 2) * (n // 2) + offset // 2) * (SLOTS + 1)
        share = dot(surf[source[i]].astype(jnp.bfloat16), weight[i])
        blocks[at + slot] = share[:fields]
        blocks[at + SLOTS, pl.ds(slot, 1), :] = jnp.full((1, columns), target_row[i].astype(jnp.float32))
        return carry

    lax.fori_loop(0, items, one, 0, unroll=items <= 16)


def corner_kernel(planes, ay, near, far, edges, place, first, second):
    even_tile = lax.axis_index("tile") % 2 == 0
    even_comp = lax.axis_index("comp") % 2 == 0
    halos = side_halos(even_tile, near[:ay, :], far[:ay, :])
    top = edges[0, :planes, :] + dot_tn(halos, place[:16, :])
    low = edges[1, :planes, :] + dot_tn(halos, place[(ay - 1) * 16 : ay * 16, :])
    first[:planes, :] = jnp.where(even_comp, low, top)
    second[:planes, :] = jnp.where(even_comp, top, low)
    first[planes:, :] = jnp.where(even_comp, edges[1, planes:, :], edges[0, planes:, :])
    second[planes:, :] = jnp.where(even_comp, edges[0, planes:, :], edges[1, planes:, :])


def side_halos(even_tile, near, far):
    left = jnp.where(even_tile, far, near)
    right = jnp.where(even_tile, near, far)
    return jnp.concatenate([left, right], axis=0).astype(jnp.bfloat16)


def finish_kernel(
    n, bands, fields, levels, olev, oy,
    atmos, ocean, near, far, first, second, shares, mix, place,
    atmos_out, ocean_out,
):
    planes, cells = fields * levels, fields * olev
    ay = atmos.shape[0] // planes
    columns = atmos.shape[1]
    me, band = lax.axis_index("tile"), lax.axis_index("comp")
    even_tile, even_comp = me % 2 == 0, band % 2 == 0
    up_all = jnp.where(even_comp, second[...], first[...])
    down_all = jnp.where(even_comp, first[...], second[...])
    rows = [row_of(atmos, k, planes, ay) for k in range(ay)]
    inner, seam = mix[:columns, :], mix[columns:, :]
    halos = side_halos(even_tile, near[:ay, :], far[:ay, :])
    across = [
        dot(rows[k].astype(jnp.bfloat16), inner)
        + dot(along_y(rows, k).astype(jnp.bfloat16), seam)
        + dot_tn(halos, place[k * 16 : (k + 1) * 16, :])
        for k in range(ay)
    ]
    for k in range(ay):
        if k % 4 == 0:
            smooth = (across[k] + (across[k - 1] if k else up_all[:planes])) * 0.5
        elif k % 4 == 3:
            smooth = (across[k] + (across[k + 1] if k + 1 < ay else down_all[:planes])) * 0.5
        else:
            smooth = across[k]
        atmos_out[pl.ds(k, planes, stride=ay), :] = rows[k] + viscosity * smooth
    lane = lax.broadcasted_iota(jnp.int32, (1, columns), 1)
    row_id = lax.broadcasted_iota(jnp.int32, (oy * cells, columns), 0)
    remapped = jnp.zeros((oy * cells, columns), jnp.float32)
    per = columns // BLOCK
    for group in range(n // per):
        ids = jnp.full((1, columns), -1.0, jnp.float32)
        for p in range(per):
            at = (group * per + p) * BLOCK
            for slot in range(SLOTS):
                here = lane // GROUP == (p * BLOCK) // GROUP + slot
                ids = jnp.where(here, shares[at + SLOTS * GROUP + slot : at + SLOTS * GROUP + slot + 1, :], ids)
        wanted = ids.astype(jnp.int32) * cells + lane % GROUP * olev
        hitting = jnp.where(row_id == wanted, 1.0, 0.0).astype(jnp.bfloat16)
        high, low = split(shares[group * columns : (group + 1) * columns, :])
        remapped = remapped + dot(hitting, high) + dot(hitting, low)
    col = lax.broadcasted_iota(jnp.int32, (cells, columns), 1)
    level = lax.broadcasted_iota(jnp.int32, (cells, columns), 0) % olev
    side = lax.broadcasted_iota(jnp.int32, (8, columns), 0)
    near_ocean, far_ocean = near[ay:, :], far[ay:, :]
    right_first = jnp.where(
        side < 4,
        jnp.where(me == n - 1, 0.0, jnp.where(even_tile, near_ocean, far_ocean)),
        jnp.where(me == 0, 0.0, jnp.where(even_tile, far_ocean, near_ocean)),
    )
    sides = jnp.concatenate(split(right_first), axis=0)
    sides_at = [dot_tn(sides, place[(ay + c) * 16 : (ay + c + 1) * 16, :]) for c in range(oy // 4)]
    cell_rows = [row_of(ocean, y, cells, oy) for y in range(oy)]
    north = jnp.where(band == 0, 0.0, up_all[planes:])
    south = jnp.where(band == bands - 1, 0.0, down_all[planes:])
    for y in range(oy):
        v = cell_rows[y]
        rolled = jnp.where(col == 0, 0.0, pltpu.roll(v, 1, 1)) + jnp.where(
            col == columns - 1, 0.0, pltpu.roll(v, columns - 1, 1)
        )
        beside = rolled + sides_at[y // 4][y % 4 * cells : (y % 4 + 1) * cells]
        above = cell_rows[y - 1] if y else north
        below = cell_rows[y + 1] if y + 1 < oy else south
        planar = below + above + beside - 4.0 * v
        upper = jnp.where(level == 0, v, pltpu.roll(v, 1, 0))
        lower = jnp.where(level == olev - 1, v, pltpu.roll(v, cells - 1, 0))
        vertical = upper + lower - 2.0 * v
        ocean_out[pl.ds(y, cells, stride=oy), :] = (
            v
            + diffusion * planar
            + mixing_rate * vertical
            + forcing_step * remapped[y * cells : (y + 1) * cells]
        )


def pair_up(count):
    return [(i, i ^ 1) for i in range(count)]


def pair_over(count):
    return [(i, (i + 1) % count if i % 2 else (i - 1) % count) for i in range(count)]


def body(mesh, atmos_state, ocean_state, flux_coef, remap_weight, source_row, target_device, target_row):
    n, bands = mesh.shape["tile"], mesh.shape["comp"]
    fields, levels, ay, columns = atmos_state.shape
    olev, oy = ocean_state.shape[1:3]
    planes, cells = fields * levels, fields * olev
    f32 = jnp.float32
    vmem = pl.BlockSpec(memory_space=pltpu.VMEM)
    smem = pl.BlockSpec(memory_space=pltpu.SMEM)
    mix, edge, place = tables(columns)
    atmos = atmos_state.reshape(planes * ay, columns)
    ocean = ocean_state.reshape(cells * oy, columns)
    params = pltpu.CompilerParams(vmem_limit_bytes=32 * 1024 * 1024)
    blocks, far_out, edges = pl.pallas_call(
        functools.partial(pack_kernel, n, fields, levels, olev, oy),
        out_shape=(
            jax.ShapeDtypeStruct((n * (SLOTS + 1) + HALO // GROUP, GROUP, columns), f32),
            jax.ShapeDtypeStruct((HALO, columns), f32),
            jax.ShapeDtypeStruct((2, planes + cells, columns), f32),
        ),
        in_specs=[smem] * 4 + [vmem] * 5,
        out_specs=(vmem, vmem, vmem),
        scratch_shapes=[pltpu.VMEM((ay, 8, columns), f32), pltpu.SMEM((n,), jnp.int32)],
        compiler_params=params,
        name="pack",
    )(flux_coef, source_row, target_device.reshape(-1), target_row, atmos, ocean, remap_weight, mix, edge)
    flat = blocks.reshape(-1, columns)
    half = n // 2 * BLOCK
    got = lax.ppermute(flat[half:], "tile", pair_up(n))
    far = lax.ppermute(far_out, "tile", pair_over(n))
    near = got[half:]
    state = jnp.concatenate(
        [flat[:half].reshape(n // 2, 1, BLOCK, columns), got[:half].reshape(n // 2, 1, BLOCK, columns)], axis=1
    )
    bit = 2
    while bit < n:
        pairs = state.reshape(state.shape[0] // 2, 2, state.shape[1], BLOCK, columns)
        came = lax.ppermute(
            pairs[:, 1].reshape(-1, columns), "tile", [(i, i ^ bit) for i in range(n)]
        ).reshape(pairs[:, 1].shape)
        state = jnp.concatenate([pairs[:, 0], came], axis=1)
        bit *= 2
    shares = state.reshape(n * BLOCK, columns)
    row_shape = jax.ShapeDtypeStruct((planes + cells, columns), f32)
    first_out, second_out = pl.pallas_call(
        functools.partial(corner_kernel, planes, ay),
        out_shape=(row_shape, row_shape),
        in_specs=[vmem] * 4,
        out_specs=(vmem, vmem),
        compiler_params=params,
        name="corners",
    )(near, far, edges, place)
    first = lax.ppermute(first_out, "comp", pair_up(bands))
    second = lax.ppermute(second_out, "comp", pair_over(bands))
    atmos_next, ocean_next = pl.pallas_call(
        functools.partial(finish_kernel, n, bands, fields, levels, olev, oy),
        out_shape=(
            jax.ShapeDtypeStruct(atmos.shape, f32),
            jax.ShapeDtypeStruct(ocean.shape, f32),
        ),
        in_specs=[vmem] * 9,
        out_specs=(vmem, vmem),
        compiler_params=params,
        name="finish",
    )(atmos, ocean, near, far, first, second, shares, mix, place)
    return atmos_next.reshape(atmos_state.shape), ocean_next.reshape(ocean_state.shape)


def solution(mesh):
    return jax.shard_map(
        functools.partial(body, mesh),
        mesh=mesh,
        in_specs=(
            P(None, None, "comp", "tile"),
            P(None, None, "comp", "tile"),
            P(),
            P(("comp", "tile"), None, None),
            P(("comp", "tile")),
            P(("comp", "tile"), None),
            P(("comp", "tile")),
        ),
        out_specs=(P(None, None, "comp", "tile"), P(None, None, "comp", "tile")),
        check_vma=False,
    )
```

```python
import functools

import jax
import jax.numpy as jnp
import numpy as np
from jax import lax
from jax.experimental import pallas as pl
from jax.experimental.pallas import tpu as pltpu
from jax.sharding import PartitionSpec as P

viscosity = 0.01
diffusion = 0.2
mixing_rate = 0.1
forcing_step = 0.5
SLOTS = 3
GROUP = 4
BLOCK = (SLOTS + 1) * GROUP
ROOMLESS = 55096 * 1024
HALO = 16


def gll_second():
    nodes = np.array([-1.0, -(0.2**0.5), 0.2**0.5, 1.0])
    derivative = np.zeros((4, 4))
    for i in range(4):
        for j in range(4):
            if i == j:
                derivative[i, j] = sum(1.0 / (nodes[i] - nodes[k]) for k in range(4) if k != i)
            else:
                top = np.prod([nodes[i] - nodes[k] for k in range(4) if k not in (i, j)])
                derivative[i, j] = top / np.prod([nodes[j] - nodes[k] for k in range(4) if k != j])
    return derivative @ derivative


def tables(columns):
    second = gll_second()
    along = np.kron(np.eye(columns // 4), second)
    seam = np.eye(columns)
    for x in range(0, columns, 4):
        for edge, other in ((x, x - 1), (x + 3, x + 4)):
            seam[edge, edge] = 0.5
            if 0 <= other < columns:
                seam[edge, other] = 0.5
    inner = (seam @ along).T
    first, last = np.eye(columns)[0], np.eye(columns)[-1]
    edge_atmos = np.zeros((16, 8 * columns))
    for k in range(8):
        for side, unit, row in ((0, first, along[0]), (8, last, along[-1])):
            edge_atmos[side + k, k * columns : (k + 1) * columns] += row
            for j in range(4):
                m = k // 4 * 4 + j
                edge_atmos[side + k, m * columns : (m + 1) * columns] += second[k % 4, j] * unit
    edge_ocean = np.zeros((16, 4 * columns))
    place_atmos = np.zeros((8, 16, columns))
    place_ocean = np.zeros((4, 16, columns))
    for c in range(4):
        edge_ocean[c, c * columns : (c + 1) * columns] = first
        edge_ocean[4 + c, c * columns : (c + 1) * columns] = last
        for part in (0, 8):
            place_ocean[c, part + c] = last
            place_ocean[c, part + 4 + c] = first
    for k in range(8):
        place_atmos[k, k] = 0.5 * first
        place_atmos[k, 8 + k] = 0.5 * last
    bf = lambda a: jnp.asarray(a.astype(np.float32)).astype(jnp.bfloat16)
    return (
        bf(np.concatenate([inner, seam.T])),
        bf(np.pad(np.concatenate([edge_atmos, edge_ocean], axis=1), ((0, 112), (0, 0)))),
        bf(np.concatenate([place_atmos.reshape(-1, columns), place_ocean.reshape(-1, columns)])),
    )


def dot(a, b):
    return jnp.dot(a, b, preferred_element_type=jnp.float32)


def dot_nt(a, b):
    return lax.dot_general(a, b, (((1,), (1,)), ((), ())), preferred_element_type=jnp.float32)


def dot_tn(a, b):
    return lax.dot_general(a, b, (((0,), (0,)), ((), ())), preferred_element_type=jnp.float32)


def split(v):
    high = v.astype(jnp.bfloat16)
    return high, (v - high.astype(jnp.float32)).astype(jnp.bfloat16)


def row_of(ref, k, count, stride):
    return ref[pl.ds(k, count, stride=stride), :]


def along_y(rows, k):
    second = gll_second()
    base = k // 4 * 4
    return sum(float(second[k % 4, j]) * rows[base + j] for j in range(4))


def edge_kernel(
    fields, levels, olev, oy, atmos_at, ocean_at, edge_at, near, far, atmos, ocean, edge, sems
):
    planes, cells = fields * levels, fields * olev
    ay = atmos.shape[0] // planes
    columns = atmos.shape[1]
    copies = [
        pltpu.make_async_copy(atmos_at, atmos, sems.at[0]),
        pltpu.make_async_copy(edge_at.at[pl.ds(0, 16), :], edge, sems.at[1]),
        pltpu.make_async_copy(ocean_at, ocean, sems.at[2]),
    ]
    for copy in copies:
        copy.start()
    even = lax.axis_index("tile") % 2 == 0
    width = ay * columns
    copies[0].wait()
    copies[1].wait()
    halves = [row_of(atmos, k, planes, ay).astype(jnp.bfloat16) for k in range(ay)]
    atmos_cols = dot_nt(edge[:, :width], jnp.concatenate(halves, axis=1))
    copies[2].wait()
    cell_rows = [row_of(ocean, y, cells, oy) for y in range(oy)]
    chunks = [jnp.concatenate(cell_rows[4 * c : 4 * c + 4], axis=0) for c in range(oy // 4)]
    parts = [split(c) for c in chunks]
    ocean_cols = dot_nt(edge[:, width:], jnp.concatenate([p[0] for p in parts], axis=1)) + dot_nt(
        edge[:, width:], jnp.concatenate([p[1] for p in parts], axis=1)
    )
    left, right = atmos_cols[:ay], atmos_cols[ay:]
    near[:ay, :] = jnp.where(even, right, left)
    far[:ay, :] = jnp.where(even, left, right)
    near[ay:, :] = ocean_cols[:8]
    far[ay:, :] = ocean_cols[:8]


def share_kernel(
    n, fields, levels, coef, source, target, target_row, atmos, weight, near,
    keep, send, surf, blocks, counts,
):
    ay = atmos.shape[0] // (fields * levels)
    columns = atmos.shape[1]
    items = weight.shape[0]
    half = n // 2 * (SLOTS + 1)
    me = lax.axis_index("tile")
    blocks[...] = jnp.full(blocks.shape, -1.0, jnp.float32)
    for y in range(ay):
        surf[y, fields:, :] = jnp.zeros((8 - fields, columns), jnp.float32)
    for f in range(fields):
        plane = atmos[f * levels * ay : f * levels * ay + ay, :] * coef[f]
        for y in range(ay):
            surf[y, f : f + 1, :] = plane[y : y + 1]

    @pl.loop(0, n)
    def _(i):
        counts[i] = 0

    def one(i, carry):
        to = target[i]
        slot = counts[to]
        counts[to] = slot + 1
        offset = to ^ me
        at = ((offset % 2) * (n // 2) + offset // 2) * (SLOTS + 1)
        share = dot(surf[source[i]].astype(jnp.bfloat16), weight[i])
        blocks[at + slot] = share[:fields]
        blocks[at + SLOTS, pl.ds(slot, 1), :] = jnp.full((1, columns), target_row[i].astype(jnp.float32))
        return carry

    lax.fori_loop(0, items, one, 0, unroll=items <= 16)
    keep[...] = blocks[:half]
    send[:half] = blocks[half:]
    for g in range(HALO // GROUP):
        send[half + g] = near[g * GROUP : (g + 1) * GROUP, :]


def corner_kernel(
    fields, levels, olev, oy, atmos, ocean, near, far, mix, place, later_in, first, second, later
):
    planes, cells = fields * levels, fields * olev
    ay = atmos.shape[0] // planes
    columns = atmos.shape[1]
    later[...] = later_in[...]
    even_tile = lax.axis_index("tile") % 2 == 0
    even_comp = lax.axis_index("comp") % 2 == 0
    halos = side_halos(even_tile, near[:ay, :], far[:ay, :])
    rows = [row_of(atmos, k, planes, ay) for k in range(ay)]
    top, low = [across_row(rows, k, mix, halos, place) for k in (0, ay - 1)]
    first[:planes, :] = jnp.where(even_comp, low, top)
    second[:planes, :] = jnp.where(even_comp, top, low)
    top, low = row_of(ocean, 0, cells, oy), row_of(ocean, oy - 1, cells, oy)
    first[planes:, :] = jnp.where(even_comp, low, top)
    second[planes:, :] = jnp.where(even_comp, top, low)


def across_row(rows, k, mix, halos, place):
    columns = mix.shape[1]
    return (
        dot(rows[k].astype(jnp.bfloat16), mix[:columns, :])
        + dot(along_y(rows, k).astype(jnp.bfloat16), mix[columns:, :])
        + dot_tn(halos, place[k * 16 : (k + 1) * 16, :])
    )


def side_halos(even_tile, near, far):
    left = jnp.where(even_tile, far, near)
    right = jnp.where(even_tile, near, far)
    return jnp.concatenate([left, right], axis=0).astype(jnp.bfloat16)


def finish_kernel(
    n, bands, fields, levels, olev, oy,
    atmos, ocean, near, far, first, second, kept, came, mix, place,
    atmos_out, ocean_out, shares,
):
    planes, cells = fields * levels, fields * olev
    ay = atmos.shape[0] // planes
    columns = atmos.shape[1]
    me, band = lax.axis_index("tile"), lax.axis_index("comp")
    even_tile, even_comp = me % 2 == 0, band % 2 == 0
    up_all = jnp.where(even_comp, second[...], first[...])
    down_all = jnp.where(even_comp, first[...], second[...])
    shares[: kept.shape[0], :] = kept[...]
    shares[kept.shape[0] :, :] = came[...]
    rows = [row_of(atmos, k, planes, ay) for k in range(ay)]
    halos = side_halos(even_tile, near[:ay, :], far[:ay, :])
    across = [across_row(rows, k, mix, halos, place) for k in range(ay)]
    for k in range(ay):
        if k % 4 == 0:
            smooth = (across[k] + (across[k - 1] if k else up_all[:planes])) * 0.5
        elif k % 4 == 3:
            smooth = (across[k] + (across[k + 1] if k + 1 < ay else down_all[:planes])) * 0.5
        else:
            smooth = across[k]
        atmos_out[pl.ds(k, planes, stride=ay), :] = rows[k] + viscosity * smooth
    lane = lax.broadcasted_iota(jnp.int32, (1, columns), 1)
    row_id = lax.broadcasted_iota(jnp.int32, (oy * cells, columns), 0)
    remapped = jnp.zeros((oy * cells, columns), jnp.float32)
    per = columns // BLOCK
    for group in range(n // per):
        ids = jnp.full((1, columns), -1.0, jnp.float32)
        for p in range(per):
            at = (group * per + p) * BLOCK
            for slot in range(SLOTS):
                here = lane // GROUP == (p * BLOCK) // GROUP + slot
                ids = jnp.where(here, shares[at + SLOTS * GROUP + slot : at + SLOTS * GROUP + slot + 1, :], ids)
        wanted = ids.astype(jnp.int32) * cells + lane % GROUP * olev
        hitting = jnp.where(row_id == wanted, 1.0, 0.0).astype(jnp.bfloat16)
        high, low = split(shares[group * columns : (group + 1) * columns, :])
        remapped = remapped + dot(hitting, high) + dot(hitting, low)
    col = lax.broadcasted_iota(jnp.int32, (cells, columns), 1)
    level = lax.broadcasted_iota(jnp.int32, (cells, columns), 0) % olev
    side = lax.broadcasted_iota(jnp.int32, (8, columns), 0)
    near_ocean, far_ocean = near[ay:, :], far[ay:, :]
    right_first = jnp.where(
        side < 4,
        jnp.where(me == n - 1, 0.0, jnp.where(even_tile, near_ocean, far_ocean)),
        jnp.where(me == 0, 0.0, jnp.where(even_tile, far_ocean, near_ocean)),
    )
    sides = jnp.concatenate(split(right_first), axis=0)
    sides_at = [dot_tn(sides, place[(ay + c) * 16 : (ay + c + 1) * 16, :]) for c in range(oy // 4)]
    cell_rows = [row_of(ocean, y, cells, oy) for y in range(oy)]
    north = jnp.where(band == 0, 0.0, up_all[planes:])
    south = jnp.where(band == bands - 1, 0.0, down_all[planes:])
    for y in range(oy):
        v = cell_rows[y]
        rolled = jnp.where(col == 0, 0.0, pltpu.roll(v, 1, 1)) + jnp.where(
            col == columns - 1, 0.0, pltpu.roll(v, columns - 1, 1)
        )
        beside = rolled + sides_at[y // 4][y % 4 * cells : (y % 4 + 1) * cells]
        above = cell_rows[y - 1] if y else north
        below = cell_rows[y + 1] if y + 1 < oy else south
        planar = below + above + beside - 4.0 * v
        upper = jnp.where(level == 0, v, pltpu.roll(v, 1, 0))
        lower = jnp.where(level == olev - 1, v, pltpu.roll(v, cells - 1, 0))
        vertical = upper + lower - 2.0 * v
        ocean_out[pl.ds(y, cells, stride=oy), :] = (
            v
            + diffusion * planar
            + mixing_rate * vertical
            + forcing_step * remapped[y * cells : (y + 1) * cells]
        )


def pair_up(count):
    return [(i, i ^ 1) for i in range(count)]


def pair_over(count):
    return [(i, (i + 1) % count if i % 2 else (i - 1) % count) for i in range(count)]


def body(mesh, atmos_state, ocean_state, flux_coef, remap_weight, source_row, target_device, target_row):
    n, bands = mesh.shape["tile"], mesh.shape["comp"]
    fields, levels, ay, columns = atmos_state.shape
    olev, oy = ocean_state.shape[1:3]
    planes, cells = fields * levels, fields * olev
    f32 = jnp.float32
    vmem = pl.BlockSpec(memory_space=pltpu.VMEM)
    smem = pl.BlockSpec(memory_space=pltpu.SMEM)
    mix, edge, place = tables(columns)
    atmos = atmos_state.reshape(planes * ay, columns)
    ocean = ocean_state.reshape(cells * oy, columns)
    params = pltpu.CompilerParams(vmem_limit_bytes=32 * 1024 * 1024)
    near_out, far_out = pl.pallas_call(
        functools.partial(edge_kernel, fields, levels, olev, oy),
        out_shape=(jax.ShapeDtypeStruct((HALO, columns), f32),) * 2,
        in_specs=[pl.BlockSpec(memory_space=pltpu.HBM)] * 3,
        out_specs=(vmem, vmem),
        scratch_shapes=[
            pltpu.VMEM(atmos.shape, f32),
            pltpu.VMEM(ocean.shape, f32),
            pltpu.VMEM((16, edge.shape[1]), jnp.bfloat16),
            pltpu.SemaphoreType.DMA((3,)),
        ],
        compiler_params=pltpu.CompilerParams(vmem_limit_bytes=ROOMLESS),
        name="edges",
    )(atmos, ocean, edge)
    far = lax.ppermute(far_out, "tile", pair_over(n))
    half = n // 2 * BLOCK
    kept, send = pl.pallas_call(
        functools.partial(share_kernel, n, fields, levels),
        out_shape=(
            jax.ShapeDtypeStruct((n // 2 * (SLOTS + 1), GROUP, columns), f32),
            jax.ShapeDtypeStruct((n // 2 * (SLOTS + 1) + HALO // GROUP, GROUP, columns), f32),
        ),
        in_specs=[smem] * 4 + [vmem] * 3,
        out_specs=(vmem, vmem),
        scratch_shapes=[
            pltpu.VMEM((ay, 8, columns), f32),
            pltpu.VMEM((n * (SLOTS + 1), GROUP, columns), f32),
            pltpu.SMEM((n,), jnp.int32),
        ],
        compiler_params=params,
        name="shares",
    )(flux_coef, source_row, target_device.reshape(-1), target_row, atmos, remap_weight, near_out)
    got = lax.ppermute(send.reshape(-1, columns), "tile", pair_up(n))
    near = got[half:]
    row_shape = jax.ShapeDtypeStruct((planes + cells, columns), f32)
    state = jnp.concatenate(
        [kept.reshape(n // 2, 1, BLOCK, columns), got[:half].reshape(n // 2, 1, BLOCK, columns)], axis=1
    )
    bit = 2
    while bit < n:
        pairs = state.reshape(state.shape[0] // 2, 2, state.shape[1], BLOCK, columns)
        keep, send = pairs[:, 0], pairs[:, 1]
        if bit == 2:
            came = lax.ppermute(send.reshape(-1, columns), "tile", [(i, i ^ bit) for i in range(n)])
            first_out, second_out, keep = pl.pallas_call(
                functools.partial(corner_kernel, fields, levels, olev, oy),
                out_shape=(row_shape, row_shape, jax.ShapeDtypeStruct((n // 2 * BLOCK, columns), f32)),
                in_specs=[vmem] * 7,
                out_specs=(vmem, vmem, vmem),
                compiler_params=params,
                name="corners",
            )(atmos, ocean, near, far, mix, place, keep.reshape(-1, columns))
            keep = keep.reshape(send.shape)
            first = lax.ppermute(first_out, "comp", pair_up(bands))
            second = lax.ppermute(second_out, "comp", pair_over(bands))
        else:
            came = lax.ppermute(send.reshape(-1, columns), "tile", [(i, i ^ bit) for i in range(n)])
        came = came.reshape(send.shape)
        state = jnp.concatenate([keep, came], axis=1)
        bit *= 2
    atmos_next, ocean_next = pl.pallas_call(
        functools.partial(finish_kernel, n, bands, fields, levels, olev, oy),
        out_shape=(
            jax.ShapeDtypeStruct(atmos.shape, f32),
            jax.ShapeDtypeStruct(ocean.shape, f32),
        ),
        in_specs=[vmem] * 10,
        out_specs=(vmem, vmem),
        scratch_shapes=[pltpu.VMEM((n * BLOCK, columns), f32)],
        compiler_params=params,
        name="finish",
    )(atmos, ocean, near, far, first, second, keep.reshape(-1, columns), came.reshape(-1, columns), mix, place)
    return atmos_next.reshape(atmos_state.shape), ocean_next.reshape(ocean_state.shape)


def solution(mesh):
    return jax.shard_map(
        functools.partial(body, mesh),
        mesh=mesh,
        in_specs=(
            P(None, None, "comp", "tile"),
            P(None, None, "comp", "tile"),
            P(),
            P(("comp", "tile"), None, None),
            P(("comp", "tile")),
            P(("comp", "tile"), None),
            P(("comp", "tile")),
        ),
        out_specs=(P(None, None, "comp", "tile"), P(None, None, "comp", "tile")),
        check_vma=False,
    )
```

```python
import functools
import math

import jax
import jax.numpy as jnp
import numpy as np
from jax import lax
from jax.experimental import pallas as pl
from jax.experimental.pallas import tpu as pltpu
from jax.sharding import PartitionSpec as P

viscosity = 0.01
diffusion = 0.2
mixing_rate = 0.1
forcing_step = 0.5
SLOTS = 3
GROUP = 4
BLOCK = (SLOTS + 1) * GROUP
ROOMLESS = 55096 * 1024
HALO = 16


def gll_second():
    nodes = np.array([-1.0, -(0.2**0.5), 0.2**0.5, 1.0])
    derivative = np.zeros((4, 4))
    for i in range(4):
        for j in range(4):
            if i == j:
                derivative[i, j] = sum(1.0 / (nodes[i] - nodes[k]) for k in range(4) if k != i)
            else:
                top = np.prod([nodes[i] - nodes[k] for k in range(4) if k not in (i, j)])
                derivative[i, j] = top / np.prod([nodes[j] - nodes[k] for k in range(4) if k != j])
    return derivative @ derivative


def tables(columns):
    second = gll_second()
    along = np.kron(np.eye(columns // 4), second)
    seam = np.eye(columns)
    for x in range(0, columns, 4):
        for edge, other in ((x, x - 1), (x + 3, x + 4)):
            seam[edge, edge] = 0.5
            if 0 <= other < columns:
                seam[edge, other] = 0.5
    inner = (seam @ along).T
    first, last = np.eye(columns)[0], np.eye(columns)[-1]
    edge_atmos = np.zeros((16, 8 * columns))
    for k in range(8):
        for side, unit, row in ((0, first, along[0]), (8, last, along[-1])):
            edge_atmos[side + k, k * columns : (k + 1) * columns] += row
            for j in range(4):
                m = k // 4 * 4 + j
                edge_atmos[side + k, m * columns : (m + 1) * columns] += second[k % 4, j] * unit
    edge_ocean = np.zeros((16, 4 * columns))
    place_atmos = np.zeros((8, 16, columns))
    place_ocean = np.zeros((4, 16, columns))
    for c in range(4):
        edge_ocean[c, c * columns : (c + 1) * columns] = first
        edge_ocean[4 + c, c * columns : (c + 1) * columns] = last
        for part in (0, 8):
            place_ocean[c, part + c] = last
            place_ocean[c, part + 4 + c] = first
    for k in range(8):
        place_atmos[k, k] = 0.5 * first
        place_atmos[k, 8 + k] = 0.5 * last
    bf = lambda a: jnp.asarray(a.astype(np.float32)).astype(jnp.bfloat16)
    return (
        bf(np.concatenate([inner, seam.T])),
        bf(np.pad(np.concatenate([edge_atmos, edge_ocean], axis=1), ((0, 112), (0, 0)))),
        bf(np.concatenate([place_atmos.reshape(-1, columns), place_ocean.reshape(-1, columns)])),
    )


def dot(a, b):
    return jnp.dot(a, b, preferred_element_type=jnp.float32)


def dot_nt(a, b):
    return lax.dot_general(a, b, (((1,), (1,)), ((), ())), preferred_element_type=jnp.float32)


def dot_tn(a, b):
    return lax.dot_general(a, b, (((0,), (0,)), ((), ())), preferred_element_type=jnp.float32)


def split(v):
    high = v.astype(jnp.bfloat16)
    return high, (v - high.astype(jnp.float32)).astype(jnp.bfloat16)


def row_of(ref, k, count, stride):
    return ref[pl.ds(k, count, stride=stride), :]


def along_y(rows, k):
    second = gll_second()
    base = k // 4 * 4
    return sum(float(second[k % 4, j]) * rows[base + j] for j in range(4))


def edge_kernel(
    fields, levels, olev, oy, atmos_at, ocean_at, edge_at, near, far, ground, atmos, ocean, edge, sems
):
    planes, cells = fields * levels, fields * olev
    ay = atmos.shape[0] // planes
    columns = atmos.shape[1]
    copies = [
        pltpu.make_async_copy(atmos_at, atmos, sems.at[0]),
        pltpu.make_async_copy(edge_at.at[pl.ds(0, 16), :], edge, sems.at[1]),
        pltpu.make_async_copy(ocean_at, ocean, sems.at[2]),
    ]
    for copy in copies:
        copy.start()
    even = lax.axis_index("tile") % 2 == 0
    width = ay * columns
    copies[0].wait()
    copies[1].wait()
    halves = [row_of(atmos, k, planes, ay).astype(jnp.bfloat16) for k in range(ay)]
    atmos_cols = dot_nt(edge[:, :width], jnp.concatenate(halves, axis=1))
    for f in range(fields):
        ground[f * ay : (f + 1) * ay, :] = atmos[f * levels * ay : f * levels * ay + ay, :]
    copies[2].wait()
    cell_rows = [row_of(ocean, y, cells, oy) for y in range(oy)]
    chunks = [jnp.concatenate(cell_rows[4 * c : 4 * c + 4], axis=0) for c in range(oy // 4)]
    parts = [split(c) for c in chunks]
    ocean_cols = dot_nt(edge[:, width:], jnp.concatenate([p[0] for p in parts], axis=1)) + dot_nt(
        edge[:, width:], jnp.concatenate([p[1] for p in parts], axis=1)
    )
    left, right = atmos_cols[:ay], atmos_cols[ay:]
    near[:ay, :] = jnp.where(even, right, left)
    far[:ay, :] = jnp.where(even, left, right)
    near[ay:, :] = ocean_cols[:8]
    far[ay:, :] = ocean_cols[:8]


def share_kernel(
    n, fields, coef_in, source_in, target_in, target_row_in, ground, weight, near,
    keep, send, coef, source, target, target_row, surf, blocks, counts, sems,
):
    copies = [
        pltpu.make_async_copy(src, dst, sems.at[place])
        for place, (src, dst) in enumerate(
            ((coef_in, coef), (source_in, source), (target_in, target), (target_row_in, target_row))
        )
    ]
    for copy in copies:
        copy.start()
    ay = ground.shape[0] // fields
    columns = ground.shape[1]
    items = weight.shape[0]
    half = n // 2 * (SLOTS + 1)
    me = lax.axis_index("tile")
    blocks[...] = jnp.full(blocks.shape, -1.0, jnp.float32)
    for y in range(ay):
        surf[y, fields:, :] = jnp.zeros((8 - fields, columns), jnp.float32)
    for copy in copies:
        copy.wait()
    for f in range(fields):
        plane = ground[f * ay : (f + 1) * ay, :] * coef[f]
        for y in range(ay):
            surf[y, f : f + 1, :] = plane[y : y + 1]

    @pl.loop(0, n)
    def _(i):
        counts[i] = 0

    def some(first, many):
        results = [
            dot(surf[source[first + i]].astype(jnp.bfloat16), weight[first + i]) for i in range(many)
        ]
        for i in range(many):
            to = target[first + i]
            slot = counts[to]
            counts[to] = slot + 1
            offset = to ^ me
            at = ((offset % 2) * (n // 2) + offset // 2) * (SLOTS + 1)
            blocks[at + slot] = results[i][:fields]
            blocks[at + SLOTS, pl.ds(slot, 1), :] = jnp.full(
                (1, columns), target_row[first + i].astype(jnp.float32)
            )

    many = math.gcd(items, 12)

    if items == many:
        some(0, many)
    else:

        @pl.loop(0, items // many)
        def _(part):
            some(part * many, many)

    keep[...] = blocks[:half]
    send[:half] = blocks[half:]
    for g in range(HALO // GROUP):
        send[half + g] = near[g * GROUP : (g + 1) * GROUP, :]


def inner_kernel(fields, levels, olev, oy, atmos, ocean, mix, atmos_part, ends, ocean_part):
    planes, cells = fields * levels, fields * olev
    ay = atmos.shape[0] // planes
    columns = atmos.shape[1]
    rows = [row_of(atmos, k, planes, ay) for k in range(ay)]
    across = [
        dot(rows[k].astype(jnp.bfloat16), mix[:columns, :])
        + dot(along_y(rows, k).astype(jnp.bfloat16), mix[columns:, :])
        for k in range(ay)
    ]
    ends[:planes, :] = across[0]
    ends[planes:, :] = across[ay - 1]
    for k in range(ay):
        smooth = sum(share * across[j] for j, share in seam_rows(ay, k))
        atmos_part[k * planes : (k + 1) * planes, :] = rows[k] + viscosity * smooth
    col = lax.broadcasted_iota(jnp.int32, (cells, columns), 1)
    level = lax.broadcasted_iota(jnp.int32, (cells, columns), 0) % olev
    cell_rows = [row_of(ocean, y, cells, oy) for y in range(oy)]
    for y in range(oy):
        v = cell_rows[y]
        planar = (
            jnp.where(col == 0, 0.0, pltpu.roll(v, 1, 1))
            + jnp.where(col == columns - 1, 0.0, pltpu.roll(v, columns - 1, 1))
            - 4.0 * v
        )
        if y:
            planar = planar + cell_rows[y - 1]
        if y + 1 < oy:
            planar = planar + cell_rows[y + 1]
        upper = jnp.where(level == 0, v, pltpu.roll(v, 1, 0))
        lower = jnp.where(level == olev - 1, v, pltpu.roll(v, cells - 1, 0))
        vertical = upper + lower - 2.0 * v
        ocean_part[y * cells : (y + 1) * cells, :] = v + diffusion * planar + mixing_rate * vertical


def seam_rows(ay, k):
    if k % 4 == 0:
        return [(k, 0.5)] + ([(k - 1, 0.5)] if k else [])
    if k % 4 == 3:
        return [(k, 0.5)] + ([(k + 1, 0.5)] if k + 1 < ay else [])
    return [(k, 1.0)]


def corner_kernel(fields, olev, oy, ocean, near, far, ends, place, later_in, first, second, later):
    cells = fields * olev
    planes = ends.shape[0] // 2
    ay = near.shape[0] - 8
    later[...] = later_in[...]
    even_tile = lax.axis_index("tile") % 2 == 0
    even_comp = lax.axis_index("comp") % 2 == 0
    halos = side_halos(even_tile, near[:ay, :], far[:ay, :])
    top = ends[:planes, :] + dot_tn(halos, place[:16, :])
    low = ends[planes:, :] + dot_tn(halos, place[(ay - 1) * 16 : ay * 16, :])
    first[:planes, :] = jnp.where(even_comp, low, top)
    second[:planes, :] = jnp.where(even_comp, top, low)
    top, low = row_of(ocean, 0, cells, oy), row_of(ocean, oy - 1, cells, oy)
    first[planes:, :] = jnp.where(even_comp, low, top)
    second[planes:, :] = jnp.where(even_comp, top, low)


def side_kernel(n, ay, oy, near, far, atmos_in, ocean_in, place, atmos_part, ocean_part):
    columns = near.shape[1]
    planes, cells = atmos_in.shape[0] // ay, ocean_in.shape[0] // oy
    me = lax.axis_index("tile")
    even_tile = me % 2 == 0
    halos = side_halos(even_tile, near[:ay, :], far[:ay, :])
    sides = [dot_tn(halos, place[k * 16 : (k + 1) * 16, :]) for k in range(ay)]
    for k in range(ay):
        here = slice(k * planes, (k + 1) * planes)
        smooth = sum(share * sides[j] for j, share in seam_rows(ay, k))
        atmos_part[here, :] = atmos_in[here, :] + viscosity * smooth
    side = lax.broadcasted_iota(jnp.int32, (8, columns), 0)
    near_ocean, far_ocean = near[ay:, :], far[ay:, :]
    right_first = jnp.where(
        side < 4,
        jnp.where(me == n - 1, 0.0, jnp.where(even_tile, near_ocean, far_ocean)),
        jnp.where(me == 0, 0.0, jnp.where(even_tile, far_ocean, near_ocean)),
    )
    parts = jnp.concatenate(split(right_first), axis=0)
    for c in range(oy // 4):
        here = slice(c * 4 * cells, (c + 1) * 4 * cells)
        four = ocean_in[here, :] + diffusion * dot_tn(
            parts, place[(ay + c) * 16 : (ay + c + 1) * 16, :]
        )
        for j in range(4):
            ocean_part[pl.ds(4 * c + j, cells, stride=oy), :] = four[j * cells : (j + 1) * cells]


def side_halos(even_tile, near, far):
    left = jnp.where(even_tile, far, near)
    right = jnp.where(even_tile, near, far)
    return jnp.concatenate([left, right], axis=0).astype(jnp.bfloat16)


def finish_kernel(
    bands, fields, levels, first, second, kept, came, atmos_part, ocean_part,
    atmos_out, ocean_out, rims, cells_out, sems,
):
    columns = atmos_part.shape[1]
    planes = fields * levels
    ay = atmos_part.shape[0] // planes
    cells = first.shape[0] - planes
    oy = ocean_part.shape[0] // cells
    olev = cells // fields
    band = lax.axis_index("comp")
    even_comp = band % 2 == 0
    copies = []

    def send(src, dst):
        copies.append(pltpu.make_async_copy(src, dst, sems.at[len(copies)]))
        copies[-1].start()

    for k in range(1, ay - 1):
        send(atmos_part.at[pl.ds(k * planes, planes), :], atmos_out.at[:, k, :])
    up = jnp.where(even_comp, second[...], first[...])
    down = jnp.where(even_comp, first[...], second[...])
    for slot, k, beyond in ((0, 0, up), (1, ay - 1, down)):
        rims[slot] = atmos_part[k * planes : (k + 1) * planes, :] + (0.5 * viscosity) * beyond[:planes]
        send(rims.at[slot], atmos_out.at[:, k, :])
    cells_out[...] = ocean_part[...]
    for y, beyond in (
        (0, jnp.where(band == 0, 0.0, up[planes:])),
        (oy - 1, jnp.where(band == bands - 1, 0.0, down[planes:])),
    ):
        row = pl.ds(y, cells, stride=oy)
        cells_out[row, :] = cells_out[row, :] + diffusion * beyond
    for f in range(fields):
        deep = pl.ds((f * olev + 1) * oy, (olev - 1) * oy)
        send(cells_out.at[deep, :], ocean_out.at[deep, :])
    lane = lax.broadcasted_iota(jnp.int32, (1, columns), 1)
    row_id = lax.broadcasted_iota(jnp.int32, (fields * oy, columns), 0)
    remapped = jnp.zeros((fields * oy, columns), jnp.float32)
    for blocks in (kept, came):
        rows = blocks.shape[0]
        for start in range(0, rows, columns):
            count = min(columns, rows - start)
            ids = jnp.full((1, columns), -float(fields * oy), jnp.float32)
            for p in range(count // BLOCK):
                at = start + p * BLOCK + SLOTS * GROUP
                for slot in range(SLOTS):
                    here = lane // GROUP == (p * BLOCK) // GROUP + slot
                    ids = jnp.where(here, blocks[at + slot : at + slot + 1, :], ids)
            wanted = jnp.where(ids < 0, -1, ids.astype(jnp.int32) + lane % GROUP * oy)
            hitting = jnp.where(row_id == wanted, forcing_step, 0.0).astype(jnp.bfloat16)[:, :count]
            high, low = split(blocks[start : start + count, :])
            remapped = remapped + dot(hitting, high) + dot(hitting, low)
    for f in range(fields):
        top = pl.ds(f * olev * oy, oy)
        cells_out[top, :] = cells_out[top, :] + remapped[f * oy : (f + 1) * oy]
        send(cells_out.at[top, :], ocean_out.at[top, :])
    for copy in copies:
        copy.wait()


def cost(flops):
    return pl.CostEstimate(flops=flops, bytes_accessed=10**6, transcendentals=0)


def pair_up(count):
    return [(i, i ^ 1) for i in range(count)]


def pair_over(count):
    return [(i, (i + 1) % count if i % 2 else (i - 1) % count) for i in range(count)]


def body(mesh, atmos_state, ocean_state, flux_coef, remap_weight, source_row, target_device, target_row):
    n, bands = mesh.shape["tile"], mesh.shape["comp"]
    fields, levels, ay, columns = atmos_state.shape
    olev, oy = ocean_state.shape[1:3]
    planes, cells = fields * levels, fields * olev
    f32 = jnp.float32
    vmem = pl.BlockSpec(memory_space=pltpu.VMEM)
    smem = pl.BlockSpec(memory_space=pltpu.SMEM)
    mix, edge, place = tables(columns)
    atmos = atmos_state.reshape(planes * ay, columns)
    ocean = ocean_state.reshape(cells * oy, columns)
    params = pltpu.CompilerParams(vmem_limit_bytes=32 * 1024 * 1024)
    near_out, far_out, ground = pl.pallas_call(
        functools.partial(edge_kernel, fields, levels, olev, oy),
        out_shape=(
            jax.ShapeDtypeStruct((HALO, columns), f32),
            jax.ShapeDtypeStruct((HALO, columns), f32),
            jax.ShapeDtypeStruct((fields * ay, columns), f32),
        ),
        in_specs=[pl.BlockSpec(memory_space=pltpu.HBM)] * 3,
        out_specs=(vmem, vmem, vmem),
        scratch_shapes=[
            pltpu.VMEM(atmos.shape, f32),
            pltpu.VMEM(ocean.shape, f32),
            pltpu.VMEM((16, edge.shape[1]), jnp.bfloat16),
            pltpu.SemaphoreType.DMA((3,)),
        ],
        compiler_params=pltpu.CompilerParams(vmem_limit_bytes=ROOMLESS),
        name="edges",
    )(atmos, ocean, edge)
    far = lax.ppermute(far_out, "tile", pair_over(n))
    half = n // 2 * BLOCK
    kept, send = pl.pallas_call(
        functools.partial(share_kernel, n, fields),
        out_shape=(
            jax.ShapeDtypeStruct((n // 2 * (SLOTS + 1), GROUP, columns), f32),
            jax.ShapeDtypeStruct((n // 2 * (SLOTS + 1) + HALO // GROUP, GROUP, columns), f32),
        ),
        in_specs=[vmem] * 7,
        out_specs=(vmem, vmem),
        scratch_shapes=[
            pltpu.SMEM(flux_coef.shape, f32),
            pltpu.SMEM(source_row.shape, jnp.int32),
            pltpu.SMEM(source_row.shape, jnp.int32),
            pltpu.SMEM(source_row.shape, jnp.int32),
            pltpu.VMEM((ay, 8, columns), f32),
            pltpu.VMEM((n * (SLOTS + 1), GROUP, columns), f32),
            pltpu.SMEM((n,), jnp.int32),
            pltpu.SemaphoreType.DMA((4,)),
        ],
        compiler_params=params,
        name="shares",
    )(flux_coef, source_row, target_device.reshape(-1), target_row, ground, remap_weight, near_out)
    got = lax.ppermute(send.reshape(-1, columns), "tile", pair_up(n))
    near = got[half:]
    row_shape = jax.ShapeDtypeStruct((planes + cells, columns), f32)
    part_shapes = jax.ShapeDtypeStruct(atmos.shape, f32), jax.ShapeDtypeStruct(ocean.shape, f32)
    atmos_part, ends, ocean_part = pl.pallas_call(
        functools.partial(inner_kernel, fields, levels, olev, oy),
        out_shape=(part_shapes[0], jax.ShapeDtypeStruct((2 * planes, columns), f32), part_shapes[1]),
        in_specs=[vmem] * 3,
        out_specs=(vmem,) * 3,
        compiler_params=params,
        cost_estimate=cost(10**9),
        name="inner",
    )(atmos, ocean, mix)
    state = jnp.concatenate(
        [kept.reshape(n // 2, 1, BLOCK, columns), got[:half].reshape(n // 2, 1, BLOCK, columns)], axis=1
    )
    bit = 2
    while bit < n:
        pairs = state.reshape(state.shape[0] // 2, 2, state.shape[1], BLOCK, columns)
        keep, send = pairs[:, 0].reshape(-1, columns), pairs[:, 1].reshape(-1, columns)
        came = lax.ppermute(send, "tile", [(i, i ^ bit) for i in range(n)])
        if bit == 2:
            first_out, second_out, keep = pl.pallas_call(
                functools.partial(corner_kernel, fields, olev, oy),
                out_shape=(
                    row_shape,
                    row_shape,
                    jax.ShapeDtypeStruct(keep.shape, f32),
                ),
                in_specs=[vmem] * 6,
                out_specs=(vmem,) * 3,
                compiler_params=params,
                cost_estimate=cost(10**9),
                name="corners",
            )(ocean, near, far, ends, place, keep)
            second = lax.ppermute(second_out, "comp", pair_over(bands))
            first = lax.ppermute(first_out, "comp", pair_up(bands))
            atmos_part, ocean_part = pl.pallas_call(
                functools.partial(side_kernel, n, ay, oy),
                out_shape=part_shapes,
                in_specs=[vmem] * 5,
                out_specs=(vmem,) * 2,
                input_output_aliases={2: 0},
                compiler_params=params,
                cost_estimate=cost(10**8),
                name="sides",
            )(near, far, atmos_part, ocean_part, place)
        state = jnp.concatenate(
            [keep.reshape(pairs[:, 0].shape), came.reshape(pairs[:, 0].shape)], axis=1
        )
        bit *= 2
    hbm = pl.BlockSpec(memory_space=pltpu.HBM)
    atmos_next, ocean_next = pl.pallas_call(
        functools.partial(finish_kernel, bands, fields, levels),
        out_shape=(jax.ShapeDtypeStruct((planes, ay, columns), f32), part_shapes[1]),
        in_specs=[vmem] * 6,
        out_specs=(hbm, hbm),
        scratch_shapes=[
            pltpu.VMEM((2, planes, columns), f32),
            pltpu.VMEM(ocean.shape, f32),
            pltpu.SemaphoreType.DMA((ay + 2 * fields,)),
        ],
        compiler_params=params,
        name="finish",
    )(first, second, keep, came, atmos_part, ocean_part)
    return atmos_next.reshape(atmos_state.shape), ocean_next.reshape(ocean_state.shape)


def solution(mesh):
    return jax.shard_map(
        functools.partial(body, mesh),
        mesh=mesh,
        in_specs=(
            P(None, None, "comp", "tile"),
            P(None, None, "comp", "tile"),
            P(),
            P(("comp", "tile"), None, None),
            P(("comp", "tile")),
            P(("comp", "tile"), None),
            P(("comp", "tile")),
        ),
        out_specs=(P(None, None, "comp", "tile"), P(None, None, "comp", "tile")),
        check_vma=False,
    )
```

```python
import functools
import math

import jax
import jax.numpy as jnp
import numpy as np
from jax import lax
from jax.experimental import pallas as pl
from jax.experimental.pallas import tpu as pltpu
from jax.sharding import PartitionSpec as P

viscosity = 0.01
diffusion = 0.2
mixing_rate = 0.1
forcing_step = 0.5
SLOTS = 3
GROUP = 4
BLOCK = (SLOTS + 1) * GROUP
ROOMLESS = 55096 * 1024
EDGES = 32
HALO = 16


def gll_second():
    nodes = np.array([-1.0, -(0.2**0.5), 0.2**0.5, 1.0])
    derivative = np.zeros((4, 4))
    for i in range(4):
        for j in range(4):
            if i == j:
                derivative[i, j] = sum(1.0 / (nodes[i] - nodes[k]) for k in range(4) if k != i)
            else:
                top = np.prod([nodes[i] - nodes[k] for k in range(4) if k not in (i, j)])
                derivative[i, j] = top / np.prod([nodes[j] - nodes[k] for k in range(4) if k != j])
    return derivative @ derivative


def tables(columns):
    second = gll_second()
    along = np.kron(np.eye(columns // 4), second)
    seam = np.eye(columns)
    for x in range(0, columns, 4):
        for edge, other in ((x, x - 1), (x + 3, x + 4)):
            seam[edge, edge] = 0.5
            if 0 <= other < columns:
                seam[edge, other] = 0.5
    inner = (seam @ along).T
    first, last = np.eye(columns)[0], np.eye(columns)[-1]
    edge_atmos = np.zeros((16, 8 * columns))
    for k in range(8):
        for side, unit, row in ((0, first, along[0]), (8, last, along[-1])):
            edge_atmos[side + k, k * columns : (k + 1) * columns] += row
            for j in range(4):
                m = k // 4 * 4 + j
                edge_atmos[side + k, m * columns : (m + 1) * columns] += second[k % 4, j] * unit
    edge_ocean = np.zeros((8, 4 * columns))
    place_atmos = np.zeros((8, 16, columns))
    place_ocean = np.zeros((4, 16, columns))
    for c in range(4):
        edge_ocean[c, c * columns : (c + 1) * columns] = first
        edge_ocean[4 + c, c * columns : (c + 1) * columns] = last
        for part in (0, 8):
            place_ocean[c, part + c] = last
            place_ocean[c, part + 4 + c] = first
    for k in range(8):
        place_atmos[k, k] = 0.5 * first
        place_atmos[k, 8 + k] = 0.5 * last
    edge = np.zeros((128, 12 * columns))
    edge[:16, : 8 * columns] = edge_atmos
    edge[16:24, 8 * columns :] = edge_ocean
    bf = lambda a: jnp.asarray(a.astype(np.float32)).astype(jnp.bfloat16)
    return (
        bf(np.concatenate([inner, seam.T])),
        bf(edge),
        bf(np.concatenate([place_atmos.reshape(-1, columns), place_ocean.reshape(-1, columns)])),
    )


def dot(a, b):
    return jnp.dot(a, b, preferred_element_type=jnp.float32)


def dot_nt(a, b):
    return lax.dot_general(a, b, (((1,), (1,)), ((), ())), preferred_element_type=jnp.float32)


def dot_tn(a, b):
    return lax.dot_general(a, b, (((0,), (0,)), ((), ())), preferred_element_type=jnp.float32)


def split(v):
    high = v.astype(jnp.bfloat16)
    return high, (v - high.astype(jnp.float32)).astype(jnp.bfloat16)


def row_of(ref, k, count, stride):
    return ref[pl.ds(k, count, stride=stride), :]


def along_y(rows, k):
    second = gll_second()
    base = k // 4 * 4
    return sum(float(second[k % 4, j]) * rows[base + j] for j in range(4))


def edge_kernel(
    fields, levels, olev, oy, atmos_at, ocean_at, edge_at, near, far, ground, atmos, ocean, edge, sems
):
    planes, cells = fields * levels, fields * olev
    ay = atmos.shape[0] // planes
    columns = atmos.shape[1]
    copies = [
        pltpu.make_async_copy(atmos_at, atmos, sems.at[0]),
        pltpu.make_async_copy(edge_at.at[pl.ds(0, EDGES), :], edge, sems.at[1]),
        pltpu.make_async_copy(ocean_at, ocean, sems.at[2]),
    ]
    for copy in copies:
        copy.start()
    even = lax.axis_index("tile") % 2 == 0
    width = ay * columns
    copies[0].wait()
    copies[1].wait()
    halves = [row_of(atmos, k, planes, ay).astype(jnp.bfloat16) for k in range(ay)]
    cols = dot_nt(jnp.concatenate(halves, axis=1), edge[:, :width])
    for f in range(fields):
        ground[f * ay : (f + 1) * ay, :] = atmos[f * levels * ay : f * levels * ay + ay, :]
    copies[2].wait()
    cell_rows = [row_of(ocean, y, cells, oy) for y in range(oy)]
    chunks = [jnp.concatenate(cell_rows[4 * c : 4 * c + 4], axis=0) for c in range(oy // 4)]
    for part in zip(*[split(c) for c in chunks]):
        cols = cols + dot_nt(jnp.concatenate(part, axis=1), edge[:, width:])
    cols = cols.T
    atmos_cols, ocean_cols = cols[: 2 * ay], cols[2 * ay : 2 * ay + 8]
    left, right = atmos_cols[:ay], atmos_cols[ay:]
    near[:ay, :] = jnp.where(even, right, left)
    far[:ay, :] = jnp.where(even, left, right)
    near[ay:, :] = ocean_cols
    far[ay:, :] = ocean_cols


def share_kernel(
    n, fields, coef_in, source_in, target_in, target_row_in, ground, weight, near,
    keep, send, surf, blocks, counts,
):
    ay = ground.shape[0] // fields
    columns = ground.shape[1]
    items = weight.shape[0]
    half = n // 2 * (SLOTS + 1)
    me = lax.axis_index("tile")
    blocks[...] = jnp.full(blocks.shape, -1.0, jnp.float32)
    for y in range(ay):
        surf[y, fields:, :] = jnp.zeros((8 - fields, columns), jnp.float32)
    coef = coef_in[...]
    source, target, target_row = source_in[...], target_in[...], target_row_in[...]
    for f in range(fields):
        plane = ground[f * ay : (f + 1) * ay, :] * coef[0, f]
        for y in range(ay):
            surf[y, f : f + 1, :] = plane[y : y + 1]

    @pl.loop(0, n)
    def _(i):
        counts[i] = 0

    def some(first, many):
        results = [
            dot(surf[source[0, first + i]].astype(jnp.bfloat16), weight[first + i]) for i in range(many)
        ]
        for i in range(many):
            to = target[0, first + i]
            slot = counts[to]
            counts[to] = slot + 1
            offset = to ^ me
            at = ((offset % 2) * (n // 2) + offset // 2) * (SLOTS + 1)
            blocks[at + slot] = results[i][:fields]
            blocks[at + SLOTS, pl.ds(slot, 1), :] = jnp.full(
                (1, columns), target_row[0, first + i].astype(jnp.float32)
            )

    many = math.gcd(items, 12)
    for part in range(items // many):
        some(part * many, many)
    keep[...] = blocks[:half]
    send[:half] = blocks[half:]
    for g in range(HALO // GROUP):
        send[half + g] = near[g * GROUP : (g + 1) * GROUP, :]


def inner_kernel(fields, levels, olev, oy, atmos, ocean, mix, atmos_part, ends, ocean_part):
    planes, cells = fields * levels, fields * olev
    ay = atmos.shape[0] // planes
    columns = atmos.shape[1]
    rows = [row_of(atmos, k, planes, ay) for k in range(ay)]
    across = [
        dot(rows[k].astype(jnp.bfloat16), mix[:columns, :])
        + dot(along_y(rows, k).astype(jnp.bfloat16), mix[columns:, :])
        for k in range(ay)
    ]
    ends[:planes, :] = across[0]
    ends[planes:, :] = across[ay - 1]
    for k in range(ay):
        smooth = sum(share * across[j] for j, share in seam_rows(ay, k))
        atmos_part[k * planes : (k + 1) * planes, :] = rows[k] + viscosity * smooth
    col = lax.broadcasted_iota(jnp.int32, (cells, columns), 1)
    level = lax.broadcasted_iota(jnp.int32, (cells, columns), 0) % olev
    cell_rows = [row_of(ocean, y, cells, oy) for y in range(oy)]
    for y in range(oy):
        v = cell_rows[y]
        planar = (
            jnp.where(col == 0, 0.0, pltpu.roll(v, 1, 1))
            + jnp.where(col == columns - 1, 0.0, pltpu.roll(v, columns - 1, 1))
            - 4.0 * v
        )
        if y:
            planar = planar + cell_rows[y - 1]
        if y + 1 < oy:
            planar = planar + cell_rows[y + 1]
        upper = jnp.where(level == 0, v, pltpu.roll(v, 1, 0))
        lower = jnp.where(level == olev - 1, v, pltpu.roll(v, cells - 1, 0))
        vertical = upper + lower - 2.0 * v
        ocean_part[y * cells : (y + 1) * cells, :] = v + diffusion * planar + mixing_rate * vertical


def seam_rows(ay, k):
    if k % 4 == 0:
        return [(k, 0.5)] + ([(k - 1, 0.5)] if k else [])
    if k % 4 == 3:
        return [(k, 0.5)] + ([(k + 1, 0.5)] if k + 1 < ay else [])
    return [(k, 1.0)]


def corner_kernel(fields, olev, oy, ocean, near, far, ends, place, later_in, low, top, later):
    cells = fields * olev
    planes = ends.shape[0] // 2
    ay = near.shape[0] - 8
    later[...] = later_in[...]
    even_tile = lax.axis_index("tile") % 2 == 0
    halos = side_halos(even_tile, near[:ay, :], far[:ay, :])
    for ref, slot, k, y in ((low, 1, ay - 1, oy - 1), (top, 0, 0, 0)):
        ref[:planes, :] = ends[slot * planes : (slot + 1) * planes, :] + dot_tn(
            halos, place[k * 16 : (k + 1) * 16, :]
        )
        ref[planes:, :] = row_of(ocean, y, cells, oy)


def side_kernel(n, ay, oy, near, far, atmos_in, ocean_in, place, atmos_part, ocean_part):
    columns = near.shape[1]
    planes, cells = atmos_in.shape[0] // ay, ocean_in.shape[0] // oy
    me = lax.axis_index("tile")
    even_tile = me % 2 == 0
    halos = side_halos(even_tile, near[:ay, :], far[:ay, :])
    sides = [dot_tn(halos, place[k * 16 : (k + 1) * 16, :]) for k in range(ay)]
    for k in range(ay):
        here = slice(k * planes, (k + 1) * planes)
        smooth = sum(share * sides[j] for j, share in seam_rows(ay, k))
        atmos_part[here, :] = atmos_in[here, :] + viscosity * smooth
    side = lax.broadcasted_iota(jnp.int32, (8, columns), 0)
    near_ocean, far_ocean = near[ay:, :], far[ay:, :]
    right_first = jnp.where(
        side < 4,
        jnp.where(me == n - 1, 0.0, jnp.where(even_tile, near_ocean, far_ocean)),
        jnp.where(me == 0, 0.0, jnp.where(even_tile, far_ocean, near_ocean)),
    )
    parts = jnp.concatenate(split(right_first), axis=0)
    for c in range(oy // 4):
        here = slice(c * 4 * cells, (c + 1) * 4 * cells)
        four = ocean_in[here, :] + diffusion * dot_tn(
            parts, place[(ay + c) * 16 : (ay + c + 1) * 16, :]
        )
        for j in range(4):
            ocean_part[pl.ds(4 * c + j, cells, stride=oy), :] = four[j * cells : (j + 1) * cells]


def side_halos(even_tile, near, far):
    left = jnp.where(even_tile, far, near)
    right = jnp.where(even_tile, near, far)
    return jnp.concatenate([left, right], axis=0).astype(jnp.bfloat16)


def finish_kernel(
    bands, fields, levels, up, came, down, kept, atmos_part, ocean_part,
    atmos_out, ocean_out, rims, cells_out, sems,
):
    columns = atmos_part.shape[1]
    planes = fields * levels
    ay = atmos_part.shape[0] // planes
    cells = up.shape[0] - planes
    oy = ocean_part.shape[0] // cells
    olev = cells // fields
    band = lax.axis_index("comp")
    copies = []

    def send(src, dst):
        copies.append(pltpu.make_async_copy(src, dst, sems.at[len(copies)]))
        copies[-1].start()

    for k in range(1, ay - 1):
        send(atmos_part.at[pl.ds(k * planes, planes), :], atmos_out.at[:, k, :])
    for slot, k, beyond in ((0, 0, up), (1, ay - 1, down)):
        rims[slot] = atmos_part[k * planes : (k + 1) * planes, :] + (0.5 * viscosity) * beyond[:planes, :]
        send(rims.at[slot], atmos_out.at[:, k, :])
    cells_out[...] = ocean_part[...]
    for y, beyond in (
        (0, jnp.where(band == 0, 0.0, up[planes:, :])),
        (oy - 1, jnp.where(band == bands - 1, 0.0, down[planes:, :])),
    ):
        row = pl.ds(y, cells, stride=oy)
        cells_out[row, :] = cells_out[row, :] + diffusion * beyond
    for f in range(fields):
        deep = pl.ds((f * olev + 1) * oy, (olev - 1) * oy)
        send(cells_out.at[deep, :], ocean_out.at[deep, :])
    lane = lax.broadcasted_iota(jnp.int32, (1, columns), 1)
    row_id = lax.broadcasted_iota(jnp.int32, (fields * oy, columns), 0)
    remapped = jnp.zeros((fields * oy, columns), jnp.float32)
    for blocks in (kept, came):
        rows = blocks.shape[0]
        for start in range(0, rows, columns):
            count = min(columns, rows - start)
            ids = jnp.full((1, columns), -float(fields * oy), jnp.float32)
            for p in range(count // BLOCK):
                at = start + p * BLOCK + SLOTS * GROUP
                for slot in range(SLOTS):
                    here = lane // GROUP == (p * BLOCK) // GROUP + slot
                    ids = jnp.where(here, blocks[at + slot : at + slot + 1, :], ids)
            wanted = jnp.where(ids < 0, -1, ids.astype(jnp.int32) + lane % GROUP * oy)
            hitting = jnp.where(row_id == wanted, forcing_step, 0.0).astype(jnp.bfloat16)[:, :count]
            high, low = split(blocks[start : start + count, :])
            remapped = remapped + dot(hitting, high) + dot(hitting, low)
    for f in range(fields):
        top = pl.ds(f * olev * oy, oy)
        cells_out[top, :] = cells_out[top, :] + remapped[f * oy : (f + 1) * oy]
        send(cells_out.at[top, :], ocean_out.at[top, :])
    for copy in copies:
        copy.wait()


def cost(flops):
    return pl.CostEstimate(flops=flops, bytes_accessed=10**6, transcendentals=0)


def pair_up(count):
    return [(i, i ^ 1) for i in range(count)]


def pair_over(count):
    return [(i, (i + 1) % count if i % 2 else (i - 1) % count) for i in range(count)]


def body(mesh, atmos_state, ocean_state, flux_coef, remap_weight, source_row, target_device, target_row):
    n, bands = mesh.shape["tile"], mesh.shape["comp"]
    fields, levels, ay, columns = atmos_state.shape
    olev, oy = ocean_state.shape[1:3]
    planes, cells = fields * levels, fields * olev
    f32 = jnp.float32
    vmem = pl.BlockSpec(memory_space=pltpu.VMEM)
    smem = pl.BlockSpec(memory_space=pltpu.SMEM)
    mix, edge, place = tables(columns)
    atmos = atmos_state.reshape(planes * ay, columns)
    ocean = ocean_state.reshape(cells * oy, columns)
    params = pltpu.CompilerParams(vmem_limit_bytes=32 * 1024 * 1024)
    near_out, far_out, ground = pl.pallas_call(
        functools.partial(edge_kernel, fields, levels, olev, oy),
        out_shape=(
            jax.ShapeDtypeStruct((HALO, columns), f32),
            jax.ShapeDtypeStruct((HALO, columns), f32),
            jax.ShapeDtypeStruct((fields * ay, columns), f32),
        ),
        in_specs=[pl.BlockSpec(memory_space=pltpu.HBM)] * 3,
        out_specs=(vmem, vmem, vmem),
        scratch_shapes=[
            pltpu.VMEM(atmos.shape, f32),
            pltpu.VMEM(ocean.shape, f32),
            pltpu.VMEM((EDGES, edge.shape[1]), jnp.bfloat16),
            pltpu.SemaphoreType.DMA((3,)),
        ],
        compiler_params=pltpu.CompilerParams(vmem_limit_bytes=ROOMLESS),
        name="edges",
    )(atmos, ocean, edge)
    far = lax.ppermute(far_out, "tile", pair_over(n))
    half = n // 2 * BLOCK
    kept, send = pl.pallas_call(
        functools.partial(share_kernel, n, fields),
        out_shape=(
            jax.ShapeDtypeStruct((n // 2 * (SLOTS + 1), GROUP, columns), f32),
            jax.ShapeDtypeStruct((n // 2 * (SLOTS + 1) + HALO // GROUP, GROUP, columns), f32),
        ),
        in_specs=[vmem] * 7,
        out_specs=(vmem, vmem),
        scratch_shapes=[
            pltpu.VMEM((ay, 8, columns), f32),
            pltpu.VMEM((n * (SLOTS + 1), GROUP, columns), f32),
            pltpu.SMEM((n,), jnp.int32),
        ],
        compiler_params=params,
        name="shares",
    )(*[a.reshape(1, -1) for a in (flux_coef, source_row, target_device, target_row)], ground, remap_weight, near_out)
    got = lax.ppermute(send.reshape(-1, columns), "tile", pair_up(n))
    near = got[half:]
    row_shape = jax.ShapeDtypeStruct((planes + cells, columns), f32)
    part_shapes = jax.ShapeDtypeStruct(atmos.shape, f32), jax.ShapeDtypeStruct(ocean.shape, f32)
    atmos_part, ends, ocean_part = pl.pallas_call(
        functools.partial(inner_kernel, fields, levels, olev, oy),
        out_shape=(part_shapes[0], jax.ShapeDtypeStruct((2 * planes, columns), f32), part_shapes[1]),
        in_specs=[vmem] * 3,
        out_specs=(vmem,) * 3,
        compiler_params=params,
        cost_estimate=cost(10**9),
        name="inner",
    )(atmos, ocean, mix)
    state = jnp.concatenate(
        [kept.reshape(n // 2, 1, BLOCK, columns), got[:half].reshape(n // 2, 1, BLOCK, columns)], axis=1
    )
    bit = 2
    while bit < n:
        pairs = state.reshape(state.shape[0] // 2, 2, state.shape[1], BLOCK, columns)
        keep, send = pairs[:, 0].reshape(-1, columns), pairs[:, 1].reshape(-1, columns)
        came = lax.ppermute(send, "tile", [(i, i ^ bit) for i in range(n)])
        if bit == 2:
            low_out, top_out, keep = pl.pallas_call(
                functools.partial(corner_kernel, fields, olev, oy),
                out_shape=(
                    row_shape,
                    row_shape,
                    jax.ShapeDtypeStruct(keep.shape, f32),
                ),
                in_specs=[vmem] * 6,
                out_specs=(vmem,) * 3,
                compiler_params=params,
                cost_estimate=cost(10**9),
                name="corners",
            )(ocean, near, far, ends, place, keep)
            up = lax.ppermute(low_out, "comp", [(i, (i + 1) % bands) for i in range(bands)])
            down = lax.ppermute(top_out, "comp", [(i, (i - 1) % bands) for i in range(bands)])
            atmos_part, ocean_part = pl.pallas_call(
                functools.partial(side_kernel, n, ay, oy),
                out_shape=part_shapes,
                in_specs=[vmem] * 5,
                out_specs=(vmem,) * 2,
                input_output_aliases={2: 0},
                compiler_params=params,
                cost_estimate=cost(10**8),
                name="sides",
            )(near, far, atmos_part, ocean_part, place)
        state = jnp.concatenate(
            [keep.reshape(pairs[:, 0].shape), came.reshape(pairs[:, 0].shape)], axis=1
        )
        bit *= 2
    hbm = pl.BlockSpec(memory_space=pltpu.HBM)
    atmos_next, ocean_next = pl.pallas_call(
        functools.partial(finish_kernel, bands, fields, levels),
        out_shape=(jax.ShapeDtypeStruct((planes, ay, columns), f32), part_shapes[1]),
        in_specs=[vmem] * 6,
        out_specs=(hbm, hbm),
        scratch_shapes=[
            pltpu.VMEM((2, planes, columns), f32),
            pltpu.VMEM(ocean.shape, f32),
            pltpu.SemaphoreType.DMA((ay + 2 * fields,)),
        ],
        compiler_params=params,
        name="finish",
    )(up, came, down, keep, atmos_part, ocean_part)
    return atmos_next.reshape(atmos_state.shape), ocean_next.reshape(ocean_state.shape)


def solution(mesh):
    return jax.shard_map(
        functools.partial(body, mesh),
        mesh=mesh,
        in_specs=(
            P(None, None, "comp", "tile"),
            P(None, None, "comp", "tile"),
            P(),
            P(("comp", "tile"), None, None),
            P(("comp", "tile")),
            P(("comp", "tile"), None),
            P(("comp", "tile")),
        ),
        out_specs=(P(None, None, "comp", "tile"), P(None, None, "comp", "tile")),
        check_vma=False,
    )
```

```python
import functools
import math

import jax
import jax.numpy as jnp
import numpy as np
from jax import lax
from jax.experimental import pallas as pl
from jax.experimental.pallas import tpu as pltpu
from jax.sharding import PartitionSpec as P

viscosity = 0.01
diffusion = 0.2
mixing_rate = 0.1
forcing_step = 0.5
SLOTS = 3
GROUP = 4
BLOCK = (SLOTS + 1) * GROUP
ROOMLESS = 55096 * 1024
EDGES = 32
HALO = 16


def gll_second():
    nodes = np.array([-1.0, -(0.2**0.5), 0.2**0.5, 1.0])
    derivative = np.zeros((4, 4))
    for i in range(4):
        for j in range(4):
            if i == j:
                derivative[i, j] = sum(1.0 / (nodes[i] - nodes[k]) for k in range(4) if k != i)
            else:
                top = np.prod([nodes[i] - nodes[k] for k in range(4) if k not in (i, j)])
                derivative[i, j] = top / np.prod([nodes[j] - nodes[k] for k in range(4) if k != j])
    return derivative @ derivative


def tables(columns):
    second = gll_second()
    along = np.kron(np.eye(columns // 4), second)
    seam = np.eye(columns)
    for x in range(0, columns, 4):
        for edge, other in ((x, x - 1), (x + 3, x + 4)):
            seam[edge, edge] = 0.5
            if 0 <= other < columns:
                seam[edge, other] = 0.5
    inner = (seam @ along).T
    first, last = np.eye(columns)[0], np.eye(columns)[-1]
    edge_atmos = np.zeros((16, 8 * columns))
    for k in range(8):
        for side, unit, row in ((0, first, along[0]), (8, last, along[-1])):
            edge_atmos[side + k, k * columns : (k + 1) * columns] += row
            for j in range(4):
                m = k // 4 * 4 + j
                edge_atmos[side + k, m * columns : (m + 1) * columns] += second[k % 4, j] * unit
    edge_ocean = np.zeros((8, 4 * columns))
    place_atmos = np.zeros((8, 16, columns))
    place_ocean = np.zeros((4, 16, columns))
    for c in range(4):
        edge_ocean[c, c * columns : (c + 1) * columns] = first
        edge_ocean[4 + c, c * columns : (c + 1) * columns] = last
        for part in (0, 8):
            place_ocean[c, part + c] = last
            place_ocean[c, part + 4 + c] = first
    for k in range(8):
        place_atmos[k, k] = 0.5 * first
        place_atmos[k, 8 + k] = 0.5 * last
    edge = np.zeros((128, 12 * columns))
    edge[:16, : 8 * columns] = edge_atmos
    edge[16:24, 8 * columns :] = edge_ocean
    bf = lambda a: jnp.asarray(a.astype(np.float32)).astype(jnp.bfloat16)
    return (
        bf(np.concatenate([inner, seam.T])),
        bf(edge),
        bf(np.concatenate([place_atmos.reshape(-1, columns), place_ocean.reshape(-1, columns)])),
    )


def dot(a, b):
    return jnp.dot(a, b, preferred_element_type=jnp.float32)


def dot_nt(a, b):
    return lax.dot_general(a, b, (((1,), (1,)), ((), ())), preferred_element_type=jnp.float32)


def dot_tn(a, b):
    return lax.dot_general(a, b, (((0,), (0,)), ((), ())), preferred_element_type=jnp.float32)


def split(v):
    high = v.astype(jnp.bfloat16)
    return high, (v - high.astype(jnp.float32)).astype(jnp.bfloat16)


def row_of(ref, k, count, stride):
    return ref[pl.ds(k, count, stride=stride), :]


def along_y(rows, k):
    second = gll_second()
    base = k // 4 * 4
    return sum(float(second[k % 4, j]) * rows[base + j] for j in range(4))


def edge_kernel(
    fields, levels, olev, oy, atmos_at, ocean_at, edge_at, near, far, ground, atmos, ocean, edge, sems
):
    planes, cells = fields * levels, fields * olev
    ay = atmos.shape[0] // planes
    columns = atmos.shape[1]
    copies = [
        pltpu.make_async_copy(atmos_at, atmos, sems.at[0]),
        pltpu.make_async_copy(edge_at.at[pl.ds(0, EDGES), :], edge, sems.at[1]),
        pltpu.make_async_copy(ocean_at, ocean, sems.at[2]),
    ]
    for copy in copies:
        copy.start()
    even = lax.axis_index("tile") % 2 == 0
    width = ay * columns
    copies[0].wait()
    copies[1].wait()
    halves = [row_of(atmos, k, planes, ay).astype(jnp.bfloat16) for k in range(ay)]
    cols = dot_nt(jnp.concatenate(halves, axis=1), edge[:, :width])
    for f in range(fields):
        ground[f * ay : (f + 1) * ay, :] = atmos[f * levels * ay : f * levels * ay + ay, :]
    copies[2].wait()
    cell_rows = [row_of(ocean, y, cells, oy) for y in range(oy)]
    chunks = [jnp.concatenate(cell_rows[4 * c : 4 * c + 4], axis=0) for c in range(oy // 4)]
    for part in zip(*[split(c) for c in chunks]):
        cols = cols + dot_nt(jnp.concatenate(part, axis=1), edge[:, width:])
    cols = cols.T
    atmos_cols, ocean_cols = cols[: 2 * ay], cols[2 * ay : 2 * ay + 8]
    left, right = atmos_cols[:ay], atmos_cols[ay:]
    near[:ay, :] = jnp.where(even, right, left)
    far[:ay, :] = jnp.where(even, left, right)
    near[ay:, :] = ocean_cols
    far[ay:, :] = ocean_cols


def share_kernel(
    n, fields, coef_in, source_in, target_in, target_row_in, ground, weight, near,
    keep, send, surf, blocks, counts,
):
    ay = ground.shape[0] // fields
    columns = ground.shape[1]
    items = weight.shape[0]
    half = n // 2 * (SLOTS + 1)
    me = lax.axis_index("tile")
    blocks[...] = jnp.full(blocks.shape, -1.0, jnp.float32)
    for y in range(ay):
        surf[y, fields:, :] = jnp.zeros((8 - fields, columns), jnp.float32)
    coef = coef_in[...]
    source, target, target_row = source_in[...], target_in[...], target_row_in[...]
    for f in range(fields):
        plane = ground[f * ay : (f + 1) * ay, :] * coef[0, f]
        for y in range(ay):
            surf[y, f : f + 1, :] = plane[y : y + 1]

    @pl.loop(0, n)
    def _(i):
        counts[i] = 0

    def some(first, many):
        results = [
            dot(surf[source[0, first + i]].astype(jnp.bfloat16), weight[first + i]) for i in range(many)
        ]
        for i in range(many):
            to = target[0, first + i]
            slot = counts[to]
            counts[to] = slot + 1
            offset = to ^ me
            at = ((offset % 2) * (n // 2) + offset // 2) * (SLOTS + 1)
            blocks[at + slot] = results[i][:fields]
            blocks[at + SLOTS, pl.ds(slot, 1), :] = jnp.full(
                (1, columns), target_row[0, first + i].astype(jnp.float32)
            )

    many = math.gcd(items, 12)
    for part in range(items // many):
        some(part * many, many)
    keep[...] = blocks[:half]
    send[:half] = blocks[half:]
    for g in range(HALO // GROUP):
        send[half + g] = near[g * GROUP : (g + 1) * GROUP, :]


def inner_kernel(fields, levels, olev, oy, atmos, ocean, mix, atmos_part, low, top, ocean_part):
    planes, cells = fields * levels, fields * olev
    ay = atmos.shape[0] // planes
    columns = atmos.shape[1]
    rows = [row_of(atmos, k, planes, ay) for k in range(ay)]
    across = [
        dot(rows[k].astype(jnp.bfloat16), mix[:columns, :])
        + dot(along_y(rows, k).astype(jnp.bfloat16), mix[columns:, :])
        for k in range(ay)
    ]
    low[:planes, :] = across[ay - 1]
    top[:planes, :] = across[0]
    for k in range(ay):
        smooth = sum(share * across[j] for j, share in seam_rows(ay, k))
        atmos_part[k * planes : (k + 1) * planes, :] = rows[k] + viscosity * smooth
    col = lax.broadcasted_iota(jnp.int32, (cells, columns), 1)
    level = lax.broadcasted_iota(jnp.int32, (cells, columns), 0) % olev
    cell_rows = [row_of(ocean, y, cells, oy) for y in range(oy)]
    low[planes:, :] = cell_rows[oy - 1]
    top[planes:, :] = cell_rows[0]
    for y in range(oy):
        v = cell_rows[y]
        planar = (
            jnp.where(col == 0, 0.0, pltpu.roll(v, 1, 1))
            + jnp.where(col == columns - 1, 0.0, pltpu.roll(v, columns - 1, 1))
            - 4.0 * v
        )
        if y:
            planar = planar + cell_rows[y - 1]
        if y + 1 < oy:
            planar = planar + cell_rows[y + 1]
        upper = jnp.where(level == 0, v, pltpu.roll(v, 1, 0))
        lower = jnp.where(level == olev - 1, v, pltpu.roll(v, cells - 1, 0))
        vertical = upper + lower - 2.0 * v
        ocean_part[y * cells : (y + 1) * cells, :] = v + diffusion * planar + mixing_rate * vertical


def seam_rows(ay, k):
    if k % 4 == 0:
        return [(k, 0.5)] + ([(k - 1, 0.5)] if k else [])
    if k % 4 == 3:
        return [(k, 0.5)] + ([(k + 1, 0.5)] if k + 1 < ay else [])
    return [(k, 1.0)]


def corner_kernel(planes, near, far, low_in, top_in, place, later_in, low, top, later):
    ay = near.shape[0] - 8
    later[...] = later_in[...]
    halos = side_halos(lax.axis_index("tile") % 2 == 0, near[:ay, :], far[:ay, :])
    for ref, old, k in ((low, low_in, ay - 1), (top, top_in, 0)):
        ref[:planes, :] = old[:planes, :] + dot_tn(halos, place[k * 16 : (k + 1) * 16, :])


def side_kernel(
    n, fields, near, far, atmos_in, ocean_in, blocks, place,
    atmos_out, rims, ocean_part, remapped, inside, sem,
):
    columns = near.shape[1]
    planes, ay = atmos_out.shape[:2]
    oy = remapped.shape[0] // fields
    cells = ocean_in.shape[0] // oy
    me = lax.axis_index("tile")
    even_tile = me % 2 == 0
    halos = side_halos(even_tile, near[:ay, :], far[:ay, :])
    sides = [dot_tn(halos, place[k * 16 : (k + 1) * 16, :]) for k in range(ay)]
    copies = []
    for k in range(ay):
        here = slice(k * planes, (k + 1) * planes)
        smooth = sum(share * sides[j] for j, share in seam_rows(ay, k))
        done = atmos_in[here, :] + viscosity * smooth
        if k in (0, ay - 1):
            rims[(planes if k else 0) : (2 * planes if k else planes), :] = done
        else:
            inside[k - 1] = done
            copies.append(pltpu.make_async_copy(inside.at[k - 1], atmos_out.at[:, k, :], sem.at[k - 1]))
            copies[-1].start()
    side = lax.broadcasted_iota(jnp.int32, (8, columns), 0)
    near_ocean, far_ocean = near[ay:, :], far[ay:, :]
    right_first = jnp.where(
        side < 4,
        jnp.where(me == n - 1, 0.0, jnp.where(even_tile, near_ocean, far_ocean)),
        jnp.where(me == 0, 0.0, jnp.where(even_tile, far_ocean, near_ocean)),
    )
    parts = jnp.concatenate(split(right_first), axis=0)
    for c in range(oy // 4):
        here = slice(c * 4 * cells, (c + 1) * 4 * cells)
        four = ocean_in[here, :] + diffusion * dot_tn(
            parts, place[(ay + c) * 16 : (ay + c + 1) * 16, :]
        )
        for j in range(4):
            ocean_part[pl.ds(4 * c + j, cells, stride=oy), :] = four[j * cells : (j + 1) * cells]
    remapped[...] = remap(blocks, fields, oy)
    for copy in copies:
        copy.wait()


def remap(blocks, fields, oy):
    rows, columns = blocks.shape
    lane = lax.broadcasted_iota(jnp.int32, (1, columns), 1)
    row_id = lax.broadcasted_iota(jnp.int32, (fields * oy, columns), 0)
    total = jnp.zeros((fields * oy, columns), jnp.float32)
    for start in range(0, rows, columns):
        count = min(columns, rows - start)
        ids = jnp.full((1, columns), -float(fields * oy), jnp.float32)
        for p in range(count // BLOCK):
            at = start + p * BLOCK + SLOTS * GROUP
            for slot in range(SLOTS):
                here = lane // GROUP == (p * BLOCK) // GROUP + slot
                ids = jnp.where(here, blocks[at + slot : at + slot + 1, :], ids)
        wanted = jnp.where(ids < 0, -1, ids.astype(jnp.int32) + lane % GROUP * oy)
        hitting = jnp.where(row_id == wanted, forcing_step, 0.0).astype(jnp.bfloat16)[:, :count]
        high, low = split(blocks[start : start + count, :])
        total = total + dot(hitting, high) + dot(hitting, low)
    return total


def side_halos(even_tile, near, far):
    left = jnp.where(even_tile, far, near)
    right = jnp.where(even_tile, near, far)
    return jnp.concatenate([left, right], axis=0).astype(jnp.bfloat16)


def finish_kernel(
    bands, fields, levels, up, came, down, atmos_so_far, rims, ocean_part, remapped,
    atmos_out, ocean_out, rims_out, cells_out, sems,
):
    planes = fields * levels
    ay = atmos_out.shape[1]
    cells = up.shape[0] - planes
    oy = ocean_part.shape[0] // cells
    olev = cells // fields
    band = lax.axis_index("comp")
    copies = []

    def send(src, dst):
        copies.append(pltpu.make_async_copy(src, dst, sems.at[len(copies)]))
        copies[-1].start()

    cells_out[...] = ocean_part[...]
    for y, beyond in (
        (0, jnp.where(band == 0, 0.0, up[planes:, :])),
        (oy - 1, jnp.where(band == bands - 1, 0.0, down[planes:, :])),
    ):
        row = pl.ds(y, cells, stride=oy)
        cells_out[row, :] = cells_out[row, :] + diffusion * beyond
    for f in range(fields):
        deep = pl.ds((f * olev + 1) * oy, (olev - 1) * oy)
        send(cells_out.at[deep, :], ocean_out.at[deep, :])
    for slot, k, beyond in ((0, 0, up), (1, ay - 1, down)):
        rims_out[slot] = (
            rims[slot * planes : (slot + 1) * planes, :] + (0.5 * viscosity) * beyond[:planes, :]
        )
        send(rims_out.at[slot], atmos_out.at[:, k, :])
    forcing = remapped[...] + remap(came, fields, oy)
    for f in range(fields):
        top = pl.ds(f * olev * oy, oy)
        cells_out[top, :] = cells_out[top, :] + forcing[f * oy : (f + 1) * oy]
        send(cells_out.at[top, :], ocean_out.at[top, :])
    for copy in copies:
        copy.wait()


def cost(flops):
    return pl.CostEstimate(flops=flops, bytes_accessed=10**6, transcendentals=0)


def pair_up(count):
    return [(i, i ^ 1) for i in range(count)]


def pair_over(count):
    return [(i, (i + 1) % count if i % 2 else (i - 1) % count) for i in range(count)]


def body(mesh, atmos_state, ocean_state, flux_coef, remap_weight, source_row, target_device, target_row):
    n, bands = mesh.shape["tile"], mesh.shape["comp"]
    fields, levels, ay, columns = atmos_state.shape
    olev, oy = ocean_state.shape[1:3]
    planes, cells = fields * levels, fields * olev
    f32 = jnp.float32
    vmem = pl.BlockSpec(memory_space=pltpu.VMEM)
    smem = pl.BlockSpec(memory_space=pltpu.SMEM)
    mix, edge, place = tables(columns)
    atmos = atmos_state.reshape(planes * ay, columns)
    ocean = ocean_state.reshape(cells * oy, columns)
    params = pltpu.CompilerParams(vmem_limit_bytes=32 * 1024 * 1024)
    near_out, far_out, ground = pl.pallas_call(
        functools.partial(edge_kernel, fields, levels, olev, oy),
        out_shape=(
            jax.ShapeDtypeStruct((HALO, columns), f32),
            jax.ShapeDtypeStruct((HALO, columns), f32),
            jax.ShapeDtypeStruct((fields * ay, columns), f32),
        ),
        in_specs=[pl.BlockSpec(memory_space=pltpu.HBM)] * 3,
        out_specs=(vmem, vmem, vmem),
        scratch_shapes=[
            pltpu.VMEM(atmos.shape, f32),
            pltpu.VMEM(ocean.shape, f32),
            pltpu.VMEM((EDGES, edge.shape[1]), jnp.bfloat16),
            pltpu.SemaphoreType.DMA((3,)),
        ],
        compiler_params=pltpu.CompilerParams(vmem_limit_bytes=ROOMLESS),
        name="edges",
    )(atmos, ocean, edge)
    far = lax.ppermute(far_out, "tile", pair_over(n))
    half = n // 2 * BLOCK
    kept, send = pl.pallas_call(
        functools.partial(share_kernel, n, fields),
        out_shape=(
            jax.ShapeDtypeStruct((n // 2 * (SLOTS + 1), GROUP, columns), f32),
            jax.ShapeDtypeStruct((n // 2 * (SLOTS + 1) + HALO // GROUP, GROUP, columns), f32),
        ),
        in_specs=[vmem] * 7,
        out_specs=(vmem, vmem),
        scratch_shapes=[
            pltpu.VMEM((ay, 8, columns), f32),
            pltpu.VMEM((n * (SLOTS + 1), GROUP, columns), f32),
            pltpu.SMEM((n,), jnp.int32),
        ],
        compiler_params=params,
        name="shares",
    )(*[a.reshape(1, -1) for a in (flux_coef, source_row, target_device, target_row)], ground, remap_weight, near_out)
    got = lax.ppermute(send.reshape(-1, columns), "tile", pair_up(n))
    near = got[half:]
    row_shape = jax.ShapeDtypeStruct((planes + cells, columns), f32)
    part_shapes = jax.ShapeDtypeStruct(atmos.shape, f32), jax.ShapeDtypeStruct(ocean.shape, f32)
    atmos_part, low, top, ocean_part = pl.pallas_call(
        functools.partial(inner_kernel, fields, levels, olev, oy),
        out_shape=(part_shapes[0], row_shape, row_shape, part_shapes[1]),
        in_specs=[vmem] * 3,
        out_specs=(vmem,) * 4,
        compiler_params=params,
        cost_estimate=cost(10**6),
        name="inner",
    )(atmos, ocean, mix)
    state = jnp.concatenate(
        [kept.reshape(n // 2, 1, BLOCK, columns), got[:half].reshape(n // 2, 1, BLOCK, columns)], axis=1
    )
    bit = 2
    while bit < n:
        pairs = state.reshape(state.shape[0] // 2, 2, state.shape[1], BLOCK, columns)
        keep, send = pairs[:, 0].reshape(-1, columns), pairs[:, 1].reshape(-1, columns)
        came = lax.ppermute(send, "tile", [(i, i ^ bit) for i in range(n)])
        if bit == 2:
            low, top, keep = pl.pallas_call(
                functools.partial(corner_kernel, planes),
                out_shape=(row_shape, row_shape, jax.ShapeDtypeStruct(keep.shape, f32)),
                in_specs=[vmem] * 6,
                out_specs=(vmem,) * 3,
                input_output_aliases={2: 0, 3: 1},
                compiler_params=params,
                cost_estimate=cost(10**9),
                name="corners",
            )(near, far, low, top, place, keep)
            up = lax.ppermute(low, "comp", [(i, (i + 1) % bands) for i in range(bands)])
            down = lax.ppermute(top, "comp", [(i, (i - 1) % bands) for i in range(bands)])
        state = jnp.concatenate(
            [keep.reshape(pairs[:, 0].shape), came.reshape(pairs[:, 0].shape)], axis=1
        )
        bit *= 2
    hbm = pl.BlockSpec(memory_space=pltpu.HBM)
    by_plane = jax.ShapeDtypeStruct((planes, ay, columns), f32)
    atmos_so_far, rims, ocean_part, remapped = pl.pallas_call(
        functools.partial(side_kernel, n, fields),
        out_shape=(
            by_plane,
            jax.ShapeDtypeStruct((2 * planes, columns), f32),
            part_shapes[1],
            jax.ShapeDtypeStruct((fields * oy, columns), f32),
        ),
        in_specs=[vmem] * 6,
        out_specs=(hbm, vmem, vmem, vmem),
        scratch_shapes=[
            pltpu.VMEM((ay - 2, planes, columns), f32),
            pltpu.SemaphoreType.DMA((ay - 2,)),
        ],
        compiler_params=params,
        cost_estimate=cost(10**8),
        name="sides",
    )(near, far, atmos_part, ocean_part, keep, place)
    atmos_next, ocean_next = pl.pallas_call(
        functools.partial(finish_kernel, bands, fields, levels),
        out_shape=(by_plane, part_shapes[1]),
        in_specs=[vmem] * 3 + [hbm] + [vmem] * 3,
        out_specs=(hbm, hbm),
        scratch_shapes=[
            pltpu.VMEM((2, planes, columns), f32),
            pltpu.VMEM(ocean.shape, f32),
            pltpu.SemaphoreType.DMA((2 + 2 * fields,)),
        ],
        input_output_aliases={3: 0},
        compiler_params=params,
        name="finish",
    )(up, came, down, atmos_so_far, rims, ocean_part, remapped)
    return atmos_next.reshape(atmos_state.shape), ocean_next.reshape(ocean_state.shape)


def solution(mesh):
    return jax.shard_map(
        functools.partial(body, mesh),
        mesh=mesh,
        in_specs=(
            P(None, None, "comp", "tile"),
            P(None, None, "comp", "tile"),
            P(),
            P(("comp", "tile"), None, None),
            P(("comp", "tile")),
            P(("comp", "tile"), None),
            P(("comp", "tile")),
        ),
        out_specs=(P(None, None, "comp", "tile"), P(None, None, "comp", "tile")),
        check_vma=False,
    )
```

```python
import functools
import math

import jax
import jax.numpy as jnp
import numpy as np
from jax import lax
from jax.experimental import pallas as pl
from jax.experimental.pallas import tpu as pltpu
from jax.sharding import PartitionSpec as P

viscosity = 0.01
diffusion = 0.2
mixing_rate = 0.1
forcing_step = 0.5
SLOTS = 3
GROUP = 4
BLOCK = (SLOTS + 1) * GROUP
ROOMLESS = 55096 * 1024
EDGES = 32
HALO = 16


def gll_second():
    nodes = np.array([-1.0, -(0.2**0.5), 0.2**0.5, 1.0])
    derivative = np.zeros((4, 4))
    for i in range(4):
        for j in range(4):
            if i == j:
                derivative[i, j] = sum(1.0 / (nodes[i] - nodes[k]) for k in range(4) if k != i)
            else:
                top = np.prod([nodes[i] - nodes[k] for k in range(4) if k not in (i, j)])
                derivative[i, j] = top / np.prod([nodes[j] - nodes[k] for k in range(4) if k != j])
    return derivative @ derivative


def tables(columns):
    second = gll_second()
    along = np.kron(np.eye(columns // 4), second)
    seam = np.eye(columns)
    for x in range(0, columns, 4):
        for edge, other in ((x, x - 1), (x + 3, x + 4)):
            seam[edge, edge] = 0.5
            if 0 <= other < columns:
                seam[edge, other] = 0.5
    inner = (seam @ along).T
    first, last = np.eye(columns)[0], np.eye(columns)[-1]
    edge_atmos = np.zeros((16, 8 * columns))
    for k in range(8):
        for side, unit, row in ((0, first, along[0]), (8, last, along[-1])):
            edge_atmos[side + k, k * columns : (k + 1) * columns] += row
            for j in range(4):
                m = k // 4 * 4 + j
                edge_atmos[side + k, m * columns : (m + 1) * columns] += second[k % 4, j] * unit
    edge_ocean = np.zeros((8, 4 * columns))
    place_atmos = np.zeros((8, 16, columns))
    place_ocean = np.zeros((4, 16, columns))
    for c in range(4):
        edge_ocean[c, c * columns : (c + 1) * columns] = first
        edge_ocean[4 + c, c * columns : (c + 1) * columns] = last
        for part in (0, 8):
            place_ocean[c, part + c] = last
            place_ocean[c, part + 4 + c] = first
    for k in range(8):
        place_atmos[k, k] = 0.5 * first
        place_atmos[k, 8 + k] = 0.5 * last
    edge = np.zeros((128, 12 * columns))
    edge[:16, : 8 * columns] = edge_atmos
    edge[16:24, 8 * columns :] = edge_ocean
    bf = lambda a: jnp.asarray(a.astype(np.float32)).astype(jnp.bfloat16)
    return (
        bf(np.concatenate([inner, seam.T])),
        bf(edge),
        bf(np.concatenate([place_atmos.reshape(-1, columns), place_ocean.reshape(-1, columns)])),
    )


def dot(a, b):
    return jnp.dot(a, b, preferred_element_type=jnp.float32)


def dot_nt(a, b):
    return lax.dot_general(a, b, (((1,), (1,)), ((), ())), preferred_element_type=jnp.float32)


def dot_tn(a, b):
    return lax.dot_general(a, b, (((0,), (0,)), ((), ())), preferred_element_type=jnp.float32)


def split(v):
    high = v.astype(jnp.bfloat16)
    return high, (v - high.astype(jnp.float32)).astype(jnp.bfloat16)


def row_of(ref, k, count, stride):
    return ref[pl.ds(k, count, stride=stride), :]


def along_y(rows, k):
    second = gll_second()
    base = k // 4 * 4
    return sum(float(second[k % 4, j]) * rows[base + j] for j in range(4))


def edge_kernel(
    fields, levels, olev, oy, atmos_at, ocean_at, edge_at, near, far, ground, atmos, ocean, edge, sems
):
    planes, cells = fields * levels, fields * olev
    ay = atmos.shape[0] // planes
    columns = atmos.shape[1]
    copies = [
        pltpu.make_async_copy(atmos_at, atmos, sems.at[0]),
        pltpu.make_async_copy(edge_at.at[pl.ds(0, EDGES), :], edge, sems.at[1]),
        pltpu.make_async_copy(ocean_at, ocean, sems.at[2]),
    ]
    for copy in copies:
        copy.start()
    even = lax.axis_index("tile") % 2 == 0
    width = ay * columns
    copies[0].wait()
    copies[1].wait()
    halves = [row_of(atmos, k, planes, ay).astype(jnp.bfloat16) for k in range(ay)]
    cols = dot_nt(jnp.concatenate(halves, axis=1), edge[:, :width])
    for f in range(fields):
        ground[f * ay : (f + 1) * ay, :] = atmos[f * levels * ay : f * levels * ay + ay, :]
    copies[2].wait()
    cell_rows = [row_of(ocean, y, cells, oy) for y in range(oy)]
    chunks = [jnp.concatenate(cell_rows[4 * c : 4 * c + 4], axis=0) for c in range(oy // 4)]
    for part in zip(*[split(c) for c in chunks]):
        cols = cols + dot_nt(jnp.concatenate(part, axis=1), edge[:, width:])
    cols = cols.T
    atmos_cols, ocean_cols = cols[: 2 * ay], cols[2 * ay : 2 * ay + 8]
    left, right = atmos_cols[:ay], atmos_cols[ay:]
    near[:ay, :] = jnp.where(even, right, left)
    far[:ay, :] = jnp.where(even, left, right)
    near[ay:, :] = ocean_cols
    far[ay:, :] = ocean_cols


def share_kernel(
    n, fields, coef_in, source_in, target_in, target_row_in, ground, weight, near,
    keep, send, surf, blocks, counts,
):
    ay = ground.shape[0] // fields
    columns = ground.shape[1]
    items = weight.shape[0]
    half = n // 2 * (SLOTS + 1)
    me = lax.axis_index("tile")
    blocks[...] = jnp.full(blocks.shape, -1.0, jnp.float32)
    for y in range(ay):
        surf[y, fields:, :] = jnp.zeros((8 - fields, columns), jnp.float32)
    coef = coef_in[...]
    source, target, target_row = source_in[...], target_in[...], target_row_in[...]
    for f in range(fields):
        plane = ground[f * ay : (f + 1) * ay, :] * coef[0, f]
        for y in range(ay):
            surf[y, f : f + 1, :] = plane[y : y + 1]

    @pl.loop(0, n)
    def _(i):
        counts[i] = 0

    def some(first, many):
        results = [
            dot(surf[source[0, first + i]].astype(jnp.bfloat16), weight[first + i]) for i in range(many)
        ]
        for i in range(many):
            to = target[0, first + i]
            slot = counts[to]
            counts[to] = slot + 1
            offset = to ^ me
            at = ((offset % 2) * (n // 2) + offset // 2) * (SLOTS + 1)
            blocks[at + slot] = results[i][:fields]
            blocks[at + SLOTS, pl.ds(slot, 1), :] = jnp.full(
                (1, columns), target_row[0, first + i].astype(jnp.float32)
            )

    many = math.gcd(items, 12)
    for part in range(items // many):
        some(part * many, many)
    keep[...] = blocks[:half]
    send[:half] = blocks[half:]
    for g in range(HALO // GROUP):
        send[half + g] = near[g * GROUP : (g + 1) * GROUP, :]


def inner_kernel(fields, levels, olev, oy, atmos, ocean, mix, atmos_part, low, top, ocean_part):
    planes, cells = fields * levels, fields * olev
    ay = atmos.shape[0] // planes
    columns = atmos.shape[1]
    rows = [row_of(atmos, k, planes, ay) for k in range(ay)]
    across = [
        dot(rows[k].astype(jnp.bfloat16), mix[:columns, :])
        + dot(along_y(rows, k).astype(jnp.bfloat16), mix[columns:, :])
        for k in range(ay)
    ]
    low[:planes, :] = across[ay - 1]
    top[:planes, :] = across[0]
    for k in range(ay):
        smooth = sum(share * across[j] for j, share in seam_rows(ay, k))
        atmos_part[k * planes : (k + 1) * planes, :] = rows[k] + viscosity * smooth
    col = lax.broadcasted_iota(jnp.int32, (cells, columns), 1)
    level = lax.broadcasted_iota(jnp.int32, (cells, columns), 0) % olev
    cell_rows = [row_of(ocean, y, cells, oy) for y in range(oy)]
    low[planes:, :] = cell_rows[oy - 1]
    top[planes:, :] = cell_rows[0]
    for y in range(oy):
        v = cell_rows[y]
        planar = (
            jnp.where(col == 0, 0.0, pltpu.roll(v, 1, 1))
            + jnp.where(col == columns - 1, 0.0, pltpu.roll(v, columns - 1, 1))
            - 4.0 * v
        )
        if y:
            planar = planar + cell_rows[y - 1]
        if y + 1 < oy:
            planar = planar + cell_rows[y + 1]
        upper = jnp.where(level == 0, v, pltpu.roll(v, 1, 0))
        lower = jnp.where(level == olev - 1, v, pltpu.roll(v, cells - 1, 0))
        vertical = upper + lower - 2.0 * v
        ocean_part[y * cells : (y + 1) * cells, :] = v + diffusion * planar + mixing_rate * vertical


def seam_rows(ay, k):
    if k % 4 == 0:
        return [(k, 0.5)] + ([(k - 1, 0.5)] if k else [])
    if k % 4 == 3:
        return [(k, 0.5)] + ([(k + 1, 0.5)] if k + 1 < ay else [])
    return [(k, 1.0)]


def corner_kernel(planes, near, far, low_in, top_in, place, later_in, low, top, later):
    ay = near.shape[0] - 8
    later[...] = later_in[...]
    halos = side_halos(lax.axis_index("tile") % 2 == 0, near[:ay, :], far[:ay, :])
    columns = place.shape[1]
    both = jnp.concatenate([place[(ay - 1) * 16 : ay * 16, :], place[:16, :]], axis=1)
    corners = dot_tn(halos, both)
    low[:planes, :] = low_in[:planes, :] + corners[:, :columns]
    top[:planes, :] = top_in[:planes, :] + corners[:, columns:]


def side_kernel(
    n, fields, near, far, atmos_in, ocean_in, blocks, place,
    atmos_out, rims, ocean_part, remapped, inside, sem,
):
    columns = near.shape[1]
    planes, ay = atmos_out.shape[:2]
    oy = remapped.shape[0] // fields
    cells = ocean_in.shape[0] // oy
    me = lax.axis_index("tile")
    even_tile = me % 2 == 0
    halos = side_halos(even_tile, near[:ay, :], far[:ay, :])
    sides = [dot_tn(halos, place[k * 16 : (k + 1) * 16, :]) for k in range(ay)]
    copies = []
    for k in range(ay):
        here = slice(k * planes, (k + 1) * planes)
        smooth = sum(share * sides[j] for j, share in seam_rows(ay, k))
        done = atmos_in[here, :] + viscosity * smooth
        if k in (0, ay - 1):
            rims[(planes if k else 0) : (2 * planes if k else planes), :] = done
        else:
            inside[k - 1] = done
            copies.append(pltpu.make_async_copy(inside.at[k - 1], atmos_out.at[:, k, :], sem.at[k - 1]))
            copies[-1].start()
    side = lax.broadcasted_iota(jnp.int32, (8, columns), 0)
    near_ocean, far_ocean = near[ay:, :], far[ay:, :]
    right_first = jnp.where(
        side < 4,
        jnp.where(me == n - 1, 0.0, jnp.where(even_tile, near_ocean, far_ocean)),
        jnp.where(me == 0, 0.0, jnp.where(even_tile, far_ocean, near_ocean)),
    )
    parts = jnp.concatenate(split(right_first), axis=0)
    for c in range(oy // 4):
        here = slice(c * 4 * cells, (c + 1) * 4 * cells)
        four = ocean_in[here, :] + diffusion * dot_tn(
            parts, place[(ay + c) * 16 : (ay + c + 1) * 16, :]
        )
        for j in range(4):
            ocean_part[pl.ds(4 * c + j, cells, stride=oy), :] = four[j * cells : (j + 1) * cells]
    remapped[...] = remap(blocks, fields, oy)
    for copy in copies:
        copy.wait()


def remap(blocks, fields, oy):
    rows, columns = blocks.shape
    lane = lax.broadcasted_iota(jnp.int32, (1, columns), 1)
    row_id = lax.broadcasted_iota(jnp.int32, (fields * oy, columns), 0)
    total = jnp.zeros((fields * oy, columns), jnp.float32)
    for start in range(0, rows, columns):
        count = min(columns, rows - start)
        ids = jnp.full((1, columns), -float(fields * oy), jnp.float32)
        for p in range(count // BLOCK):
            at = start + p * BLOCK + SLOTS * GROUP
            for slot in range(SLOTS):
                here = lane // GROUP == (p * BLOCK) // GROUP + slot
                ids = jnp.where(here, blocks[at + slot : at + slot + 1, :], ids)
        wanted = jnp.where(ids < 0, -1, ids.astype(jnp.int32) + lane % GROUP * oy)
        hitting = jnp.where(row_id == wanted, forcing_step, 0.0).astype(jnp.bfloat16)[:, :count]
        high, low = split(blocks[start : start + count, :])
        total = total + dot(hitting, high) + dot(hitting, low)
    return total


def side_halos(even_tile, near, far):
    left = jnp.where(even_tile, far, near)
    right = jnp.where(even_tile, near, far)
    return jnp.concatenate([left, right], axis=0).astype(jnp.bfloat16)


def finish_kernel(
    bands, fields, levels, up, came, down, atmos_so_far, rims, ocean_part, remapped,
    atmos_out, ocean_out, rims_out, cells_out, sems,
):
    planes = fields * levels
    ay = atmos_out.shape[1]
    cells = up.shape[0] - planes
    oy = ocean_part.shape[0] // cells
    olev = cells // fields
    band = lax.axis_index("comp")
    copies = []

    def send(src, dst):
        copies.append(pltpu.make_async_copy(src, dst, sems.at[len(copies)]))
        copies[-1].start()

    for slot, k, beyond in ((0, 0, up), (1, ay - 1, down)):
        rims_out[slot] = (
            rims[slot * planes : (slot + 1) * planes, :] + (0.5 * viscosity) * beyond[:planes, :]
        )
        send(rims_out.at[slot], atmos_out.at[:, k, :])
    cells_out[...] = ocean_part[...]
    for y, beyond in (
        (0, jnp.where(band == 0, 0.0, up[planes:, :])),
        (oy - 1, jnp.where(band == bands - 1, 0.0, down[planes:, :])),
    ):
        row = pl.ds(y, cells, stride=oy)
        cells_out[row, :] = cells_out[row, :] + diffusion * beyond
    for f in range(fields):
        deep = pl.ds((f * olev + 1) * oy, (olev - 1) * oy)
        send(cells_out.at[deep, :], ocean_out.at[deep, :])
    forcing = remapped[...] + remap(came, fields, oy)
    for f in range(fields):
        top = pl.ds(f * olev * oy, oy)
        cells_out[top, :] = cells_out[top, :] + forcing[f * oy : (f + 1) * oy]
        send(cells_out.at[top, :], ocean_out.at[top, :])
    for copy in copies:
        copy.wait()


def cost(flops):
    return pl.CostEstimate(flops=flops, bytes_accessed=10**6, transcendentals=0)


def pair_up(count):
    return [(i, i ^ 1) for i in range(count)]


def pair_over(count):
    return [(i, (i + 1) % count if i % 2 else (i - 1) % count) for i in range(count)]


def body(mesh, atmos_state, ocean_state, flux_coef, remap_weight, source_row, target_device, target_row):
    n, bands = mesh.shape["tile"], mesh.shape["comp"]
    fields, levels, ay, columns = atmos_state.shape
    olev, oy = ocean_state.shape[1:3]
    planes, cells = fields * levels, fields * olev
    f32 = jnp.float32
    vmem = pl.BlockSpec(memory_space=pltpu.VMEM)
    smem = pl.BlockSpec(memory_space=pltpu.SMEM)
    mix, edge, place = tables(columns)
    atmos = atmos_state.reshape(planes * ay, columns)
    ocean = ocean_state.reshape(cells * oy, columns)
    params = pltpu.CompilerParams(vmem_limit_bytes=32 * 1024 * 1024)
    near_out, far_out, ground = pl.pallas_call(
        functools.partial(edge_kernel, fields, levels, olev, oy),
        out_shape=(
            jax.ShapeDtypeStruct((HALO, columns), f32),
            jax.ShapeDtypeStruct((HALO, columns), f32),
            jax.ShapeDtypeStruct((fields * ay, columns), f32),
        ),
        in_specs=[pl.BlockSpec(memory_space=pltpu.HBM)] * 3,
        out_specs=(vmem, vmem, vmem),
        scratch_shapes=[
            pltpu.VMEM(atmos.shape, f32),
            pltpu.VMEM(ocean.shape, f32),
            pltpu.VMEM((EDGES, edge.shape[1]), jnp.bfloat16),
            pltpu.SemaphoreType.DMA((3,)),
        ],
        compiler_params=pltpu.CompilerParams(vmem_limit_bytes=ROOMLESS),
        name="edges",
    )(atmos, ocean, edge)
    far = lax.ppermute(far_out, "tile", pair_over(n))
    half = n // 2 * BLOCK
    kept, send = pl.pallas_call(
        functools.partial(share_kernel, n, fields),
        out_shape=(
            jax.ShapeDtypeStruct((n // 2 * (SLOTS + 1), GROUP, columns), f32),
            jax.ShapeDtypeStruct((n // 2 * (SLOTS + 1) + HALO // GROUP, GROUP, columns), f32),
        ),
        in_specs=[vmem] * 7,
        out_specs=(vmem, vmem),
        scratch_shapes=[
            pltpu.VMEM((ay, 8, columns), f32),
            pltpu.VMEM((n * (SLOTS + 1), GROUP, columns), f32),
            pltpu.SMEM((n,), jnp.int32),
        ],
        compiler_params=params,
        name="shares",
    )(*[a.reshape(1, -1) for a in (flux_coef, source_row, target_device, target_row)], ground, remap_weight, near_out)
    got = lax.ppermute(send.reshape(-1, columns), "tile", pair_up(n))
    near = got[half:]
    row_shape = jax.ShapeDtypeStruct((planes + cells, columns), f32)
    part_shapes = jax.ShapeDtypeStruct(atmos.shape, f32), jax.ShapeDtypeStruct(ocean.shape, f32)
    atmos_part, low, top, ocean_part = pl.pallas_call(
        functools.partial(inner_kernel, fields, levels, olev, oy),
        out_shape=(part_shapes[0], row_shape, row_shape, part_shapes[1]),
        in_specs=[vmem] * 3,
        out_specs=(vmem,) * 4,
        compiler_params=params,
        cost_estimate=cost(10**6),
        name="inner",
    )(atmos, ocean, mix)
    state = jnp.concatenate(
        [kept.reshape(n // 2, 1, BLOCK, columns), got[:half].reshape(n // 2, 1, BLOCK, columns)], axis=1
    )
    bit = 2
    while bit < n:
        pairs = state.reshape(state.shape[0] // 2, 2, state.shape[1], BLOCK, columns)
        keep, send = pairs[:, 0].reshape(-1, columns), pairs[:, 1].reshape(-1, columns)
        came = lax.ppermute(send, "tile", [(i, i ^ bit) for i in range(n)])
        if bit == 2:
            low, top, keep = pl.pallas_call(
                functools.partial(corner_kernel, planes),
                out_shape=(row_shape, row_shape, jax.ShapeDtypeStruct(keep.shape, f32)),
                in_specs=[vmem] * 6,
                out_specs=(vmem,) * 3,
                input_output_aliases={2: 0, 3: 1},
                compiler_params=params,
                cost_estimate=cost(10**9),
                name="corners",
            )(near, far, low, top, place, keep)
            up = lax.ppermute(low, "comp", [(i, (i + 1) % bands) for i in range(bands)])
            down = lax.ppermute(top, "comp", [(i, (i - 1) % bands) for i in range(bands)])
        state = jnp.concatenate(
            [keep.reshape(pairs[:, 0].shape), came.reshape(pairs[:, 0].shape)], axis=1
        )
        bit *= 2
    hbm = pl.BlockSpec(memory_space=pltpu.HBM)
    by_plane = jax.ShapeDtypeStruct((planes, ay, columns), f32)
    atmos_so_far, rims, ocean_part, remapped = pl.pallas_call(
        functools.partial(side_kernel, n, fields),
        out_shape=(
            by_plane,
            jax.ShapeDtypeStruct((2 * planes, columns), f32),
            part_shapes[1],
            jax.ShapeDtypeStruct((fields * oy, columns), f32),
        ),
        in_specs=[vmem] * 6,
        out_specs=(hbm, vmem, vmem, vmem),
        scratch_shapes=[
            pltpu.VMEM((ay - 2, planes, columns), f32),
            pltpu.SemaphoreType.DMA((ay - 2,)),
        ],
        compiler_params=params,
        cost_estimate=cost(10**8),
        name="sides",
    )(near, far, atmos_part, ocean_part, keep, place)
    atmos_next, ocean_next = pl.pallas_call(
        functools.partial(finish_kernel, bands, fields, levels),
        out_shape=(by_plane, part_shapes[1]),
        in_specs=[vmem] * 3 + [hbm] + [vmem] * 3,
        out_specs=(hbm, hbm),
        scratch_shapes=[
            pltpu.VMEM((2, planes, columns), f32),
            pltpu.VMEM(ocean.shape, f32),
            pltpu.SemaphoreType.DMA((2 + 2 * fields,)),
        ],
        input_output_aliases={3: 0},
        compiler_params=params,
        name="finish",
    )(up, came, down, atmos_so_far, rims, ocean_part, remapped)
    return atmos_next.reshape(atmos_state.shape), ocean_next.reshape(ocean_state.shape)


def solution(mesh):
    return jax.shard_map(
        functools.partial(body, mesh),
        mesh=mesh,
        in_specs=(
            P(None, None, "comp", "tile"),
            P(None, None, "comp", "tile"),
            P(),
            P(("comp", "tile"), None, None),
            P(("comp", "tile")),
            P(("comp", "tile"), None),
            P(("comp", "tile")),
        ),
        out_specs=(P(None, None, "comp", "tile"), P(None, None, "comp", "tile")),
        check_vma=False,
    )
```

```python
import functools
import math

import jax
import jax.numpy as jnp
import numpy as np
from jax import lax
from jax.experimental import pallas as pl
from jax.experimental.pallas import tpu as pltpu
from jax.sharding import PartitionSpec as P

viscosity = 0.01
diffusion = 0.2
mixing_rate = 0.1
forcing_step = 0.5
SLOTS = 3
GROUP = 4
BLOCK = (SLOTS + 1) * GROUP
ROOMLESS = 55096 * 1024
EDGES = 32
HALO = 16


def gll_second():
    nodes = np.array([-1.0, -(0.2**0.5), 0.2**0.5, 1.0])
    derivative = np.zeros((4, 4))
    for i in range(4):
        for j in range(4):
            if i == j:
                derivative[i, j] = sum(1.0 / (nodes[i] - nodes[k]) for k in range(4) if k != i)
            else:
                top = np.prod([nodes[i] - nodes[k] for k in range(4) if k not in (i, j)])
                derivative[i, j] = top / np.prod([nodes[j] - nodes[k] for k in range(4) if k != j])
    return derivative @ derivative


def tables(columns):
    second = gll_second()
    along = np.kron(np.eye(columns // 4), second)
    seam = np.eye(columns)
    for x in range(0, columns, 4):
        for edge, other in ((x, x - 1), (x + 3, x + 4)):
            seam[edge, edge] = 0.5
            if 0 <= other < columns:
                seam[edge, other] = 0.5
    inner = (seam @ along).T
    first, last = np.eye(columns)[0], np.eye(columns)[-1]
    edge_atmos = np.zeros((16, 8 * columns))
    for k in range(8):
        for side, unit, row in ((0, first, along[0]), (8, last, along[-1])):
            edge_atmos[side + k, k * columns : (k + 1) * columns] += row
            for j in range(4):
                m = k // 4 * 4 + j
                edge_atmos[side + k, m * columns : (m + 1) * columns] += second[k % 4, j] * unit
    edge_ocean = np.zeros((8, 4 * columns))
    place_atmos = np.zeros((8, 16, columns))
    place_ocean = np.zeros((4, 16, columns))
    for c in range(4):
        edge_ocean[c, c * columns : (c + 1) * columns] = first
        edge_ocean[4 + c, c * columns : (c + 1) * columns] = last
        for part in (0, 8):
            place_ocean[c, part + c] = last
            place_ocean[c, part + 4 + c] = first
    for k in range(8):
        place_atmos[k, k] = 0.5 * first
        place_atmos[k, 8 + k] = 0.5 * last
    edge = np.zeros((128, 12 * columns))
    edge[:16, : 8 * columns] = edge_atmos
    edge[16:24, 8 * columns :] = edge_ocean
    bf = lambda a: jnp.asarray(a.astype(np.float32)).astype(jnp.bfloat16)
    return (
        bf(np.concatenate([inner, seam.T])),
        bf(edge),
        bf(np.concatenate([place_atmos.reshape(-1, columns), place_ocean.reshape(-1, columns)])),
    )


def dot(a, b):
    return jnp.dot(a, b, preferred_element_type=jnp.float32)


def dot_nt(a, b):
    return lax.dot_general(a, b, (((1,), (1,)), ((), ())), preferred_element_type=jnp.float32)


def dot_tn(a, b):
    return lax.dot_general(a, b, (((0,), (0,)), ((), ())), preferred_element_type=jnp.float32)


def split(v):
    high = v.astype(jnp.bfloat16)
    return high, (v - high.astype(jnp.float32)).astype(jnp.bfloat16)


def row_of(ref, k, count, stride):
    return ref[pl.ds(k, count, stride=stride), :]


def along_y(rows, k):
    second = gll_second()
    base = k // 4 * 4
    return sum(float(second[k % 4, j]) * rows[base + j] for j in range(4))


def edge_kernel(
    fields, levels, olev, oy, atmos_at, ocean_at, edge_at, near, far, ground, atmos, ocean, edge, sems
):
    planes, cells = fields * levels, fields * olev
    ay = atmos.shape[0] // planes
    columns = atmos.shape[1]
    copies = [
        pltpu.make_async_copy(atmos_at, atmos, sems.at[0]),
        pltpu.make_async_copy(edge_at.at[pl.ds(0, EDGES), :], edge, sems.at[1]),
        pltpu.make_async_copy(ocean_at, ocean, sems.at[2]),
    ]
    for copy in copies:
        copy.start()
    even = lax.axis_index("tile") % 2 == 0
    width = ay * columns
    copies[0].wait()
    copies[1].wait()
    halves = [row_of(atmos, k, planes, ay).astype(jnp.bfloat16) for k in range(ay)]
    cols = dot_nt(jnp.concatenate(halves, axis=1), edge[:, :width])
    for f in range(fields):
        ground[f * ay : (f + 1) * ay, :] = atmos[f * levels * ay : f * levels * ay + ay, :]
    copies[2].wait()
    cell_rows = [row_of(ocean, y, cells, oy) for y in range(oy)]
    chunks = [jnp.concatenate(cell_rows[4 * c : 4 * c + 4], axis=0) for c in range(oy // 4)]
    for part in zip(*[split(c) for c in chunks]):
        cols = cols + dot_nt(jnp.concatenate(part, axis=1), edge[:, width:])
    cols = cols.T
    atmos_cols, ocean_cols = cols[: 2 * ay], cols[2 * ay : 2 * ay + 8]
    left, right = atmos_cols[:ay], atmos_cols[ay:]
    near[:ay, :] = jnp.where(even, right, left)
    far[:ay, :] = jnp.where(even, left, right)
    near[ay:, :] = ocean_cols
    far[ay:, :] = ocean_cols


def share_kernel(
    n, fields, coef_in, source_in, target_in, target_row_in, ground, weight, near,
    keep, send, surf, blocks, counts,
):
    ay = ground.shape[0] // fields
    columns = ground.shape[1]
    items = weight.shape[0]
    half = n // 2 * (SLOTS + 1)
    me = lax.axis_index("tile")
    blocks[...] = jnp.full(blocks.shape, -1.0, jnp.float32)
    for y in range(ay):
        surf[y, fields:, :] = jnp.zeros((8 - fields, columns), jnp.float32)
    coef = coef_in[...]
    source, target, target_row = source_in[...], target_in[...], target_row_in[...]
    for f in range(fields):
        plane = ground[f * ay : (f + 1) * ay, :] * coef[0, f]
        for y in range(ay):
            surf[y, f : f + 1, :] = plane[y : y + 1]

    @pl.loop(0, n)
    def _(i):
        counts[i] = 0

    def some(first, many):
        results = [
            dot(surf[source[0, first + i]].astype(jnp.bfloat16), weight[first + i]) for i in range(many)
        ]
        for i in range(many):
            to = target[0, first + i]
            slot = counts[to]
            counts[to] = slot + 1
            offset = to ^ me
            at = ((offset % 2) * (n // 2) + offset // 2) * (SLOTS + 1)
            blocks[at + slot] = results[i][:fields]
            blocks[at + SLOTS, pl.ds(slot, 1), :] = jnp.full(
                (1, columns), target_row[0, first + i].astype(jnp.float32)
            )

    many = math.gcd(items, 12)
    for part in range(items // many):
        some(part * many, many)
    keep[...] = blocks[:half]
    send[:half] = blocks[half:]
    for g in range(HALO // GROUP):
        send[half + g] = near[g * GROUP : (g + 1) * GROUP, :]


def inner_kernel(fields, levels, olev, oy, atmos, ocean, mix, atmos_part, low, top, ocean_part):
    planes, cells = fields * levels, fields * olev
    ay = atmos.shape[0] // planes
    columns = atmos.shape[1]
    rows = [row_of(atmos, k, planes, ay) for k in range(ay)]
    across = [
        dot(rows[k].astype(jnp.bfloat16), mix[:columns, :])
        + dot(along_y(rows, k).astype(jnp.bfloat16), mix[columns:, :])
        for k in range(ay)
    ]
    low[:planes, :] = across[ay - 1]
    top[:planes, :] = across[0]
    for k in range(ay):
        smooth = sum(share * across[j] for j, share in seam_rows(ay, k))
        atmos_part[k * planes : (k + 1) * planes, :] = rows[k] + viscosity * smooth
    col = lax.broadcasted_iota(jnp.int32, (cells, columns), 1)
    level = lax.broadcasted_iota(jnp.int32, (cells, columns), 0) % olev
    cell_rows = [row_of(ocean, y, cells, oy) for y in range(oy)]
    low[planes:, :] = cell_rows[oy - 1]
    top[planes:, :] = cell_rows[0]
    for y in range(oy):
        v = cell_rows[y]
        planar = (
            jnp.where(col == 0, 0.0, pltpu.roll(v, 1, 1))
            + jnp.where(col == columns - 1, 0.0, pltpu.roll(v, columns - 1, 1))
            - 4.0 * v
        )
        if y:
            planar = planar + cell_rows[y - 1]
        if y + 1 < oy:
            planar = planar + cell_rows[y + 1]
        upper = jnp.where(level == 0, v, pltpu.roll(v, 1, 0))
        lower = jnp.where(level == olev - 1, v, pltpu.roll(v, cells - 1, 0))
        vertical = upper + lower - 2.0 * v
        ocean_part[y * cells : (y + 1) * cells, :] = v + diffusion * planar + mixing_rate * vertical


def seam_rows(ay, k):
    if k % 4 == 0:
        return [(k, 0.5)] + ([(k - 1, 0.5)] if k else [])
    if k % 4 == 3:
        return [(k, 0.5)] + ([(k + 1, 0.5)] if k + 1 < ay else [])
    return [(k, 1.0)]


def corner_kernel(planes, near, far, low_in, top_in, place, later_in, low, top, later):
    ay = near.shape[0] - 8
    later[...] = later_in[...]
    halos = side_halos(lax.axis_index("tile") % 2 == 0, near[:ay, :], far[:ay, :])
    columns = place.shape[1]
    both = jnp.concatenate([place[(ay - 1) * 16 : ay * 16, :], place[:16, :]], axis=1)
    corners = dot_tn(halos, both)
    low[:planes, :] = low_in[:planes, :] + corners[:, :columns]
    top[:planes, :] = top_in[:planes, :] + corners[:, columns:]


def side_kernel(
    n, fields, near, far, atmos_in, ocean_in, blocks, place,
    atmos_out, rims, ocean_part, remapped, inside, sem,
):
    columns = near.shape[1]
    planes, ay = atmos_out.shape[:2]
    oy = remapped.shape[0] // fields
    cells = ocean_in.shape[0] // oy
    me = lax.axis_index("tile")
    even_tile = me % 2 == 0
    halos = side_halos(even_tile, near[:ay, :], far[:ay, :])
    sides = [dot_tn(halos, place[k * 16 : (k + 1) * 16, :]) for k in range(ay)]
    copies = []
    for k in range(ay):
        here = slice(k * planes, (k + 1) * planes)
        smooth = sum(share * sides[j] for j, share in seam_rows(ay, k))
        done = atmos_in[here, :] + viscosity * smooth
        if k in (0, ay - 1):
            rims[(planes if k else 0) : (2 * planes if k else planes), :] = done
        else:
            inside[k - 1] = done
            copies.append(pltpu.make_async_copy(inside.at[k - 1], atmos_out.at[:, k, :], sem.at[k - 1]))
            copies[-1].start()
    side = lax.broadcasted_iota(jnp.int32, (8, columns), 0)
    near_ocean, far_ocean = near[ay:, :], far[ay:, :]
    right_first = jnp.where(
        side < 4,
        jnp.where(me == n - 1, 0.0, jnp.where(even_tile, near_ocean, far_ocean)),
        jnp.where(me == 0, 0.0, jnp.where(even_tile, far_ocean, near_ocean)),
    )
    parts = jnp.concatenate(split(right_first), axis=0)
    for c in range(oy // 4):
        here = slice(c * 4 * cells, (c + 1) * 4 * cells)
        four = ocean_in[here, :] + diffusion * dot_tn(
            parts, place[(ay + c) * 16 : (ay + c + 1) * 16, :]
        )
        for j in range(4):
            ocean_part[pl.ds(4 * c + j, cells, stride=oy), :] = four[j * cells : (j + 1) * cells]
    remapped[...] = remap(blocks, fields, oy)
    for copy in copies:
        copy.wait()


def remap(blocks, fields, oy):
    rows, columns = blocks.shape
    lane = lax.broadcasted_iota(jnp.int32, (1, columns), 1)
    row_id = lax.broadcasted_iota(jnp.int32, (fields * oy, columns), 0)
    total = jnp.zeros((fields * oy, columns), jnp.float32)
    for start in range(0, rows, columns):
        count = min(columns, rows - start)
        ids = jnp.full((1, columns), -float(fields * oy), jnp.float32)
        for p in range(count // BLOCK):
            at = start + p * BLOCK + SLOTS * GROUP
            for slot in range(SLOTS):
                here = lane // GROUP == (p * BLOCK) // GROUP + slot
                ids = jnp.where(here, blocks[at + slot : at + slot + 1, :], ids)
        wanted = jnp.where(ids < 0, -1, ids.astype(jnp.int32) + lane % GROUP * oy)
        hitting = jnp.where(row_id == wanted, forcing_step, 0.0).astype(jnp.bfloat16)[:, :count]
        high, low = split(blocks[start : start + count, :])
        total = total + dot(hitting, high) + dot(hitting, low)
    return total


def side_halos(even_tile, near, far):
    left = jnp.where(even_tile, far, near)
    right = jnp.where(even_tile, near, far)
    return jnp.concatenate([left, right], axis=0).astype(jnp.bfloat16)


def finish_kernel(
    bands, fields, levels, up, came, down, atmos_so_far, rims, ocean_part, remapped,
    atmos_out, ocean_out, rims_out, cells_out, sems,
):
    planes = fields * levels
    ay = atmos_out.shape[1]
    cells = up.shape[0] - planes
    oy = ocean_part.shape[0] // cells
    olev = cells // fields
    band = lax.axis_index("comp")
    copies = []

    def send(src, dst):
        copies.append(pltpu.make_async_copy(src, dst, sems.at[len(copies)]))
        copies[-1].start()

    for slot, k, beyond in ((0, 0, up), (1, ay - 1, down)):
        rims_out[slot] = (
            rims[slot * planes : (slot + 1) * planes, :] + (0.5 * viscosity) * beyond[:planes, :]
        )
        send(rims_out.at[slot], atmos_out.at[:, k, :])
    for f in range(fields):
        cells_out[f] = ocean_part[f * olev * oy : (f + 1) * olev * oy, :]
    for y, beyond in (
        (0, jnp.where(band == 0, 0.0, up[planes:, :])),
        (oy - 1, jnp.where(band == bands - 1, 0.0, down[planes:, :])),
    ):
        row = pl.ds(y, olev, stride=oy)
        for f in range(fields):
            cells_out[f, row, :] = cells_out[f, row, :] + diffusion * beyond[f * olev : (f + 1) * olev]
    deep = pl.ds(oy, (olev - 1) * oy)
    send(cells_out.at[:, deep, :], ocean_out.at[:, deep, :])
    forcing = remapped[...] + remap(came, fields, oy)
    for f in range(fields):
        cells_out[f, :oy, :] = cells_out[f, :oy, :] + forcing[f * oy : (f + 1) * oy]
    top = pl.ds(0, oy)
    send(cells_out.at[:, top, :], ocean_out.at[:, top, :])
    for copy in copies:
        copy.wait()


def cost(flops):
    return pl.CostEstimate(flops=flops, bytes_accessed=10**6, transcendentals=0)


def pair_up(count):
    return [(i, i ^ 1) for i in range(count)]


def pair_over(count):
    return [(i, (i + 1) % count if i % 2 else (i - 1) % count) for i in range(count)]


def body(mesh, atmos_state, ocean_state, flux_coef, remap_weight, source_row, target_device, target_row):
    n, bands = mesh.shape["tile"], mesh.shape["comp"]
    fields, levels, ay, columns = atmos_state.shape
    olev, oy = ocean_state.shape[1:3]
    planes, cells = fields * levels, fields * olev
    f32 = jnp.float32
    vmem = pl.BlockSpec(memory_space=pltpu.VMEM)
    smem = pl.BlockSpec(memory_space=pltpu.SMEM)
    mix, edge, place = tables(columns)
    atmos = atmos_state.reshape(planes * ay, columns)
    ocean = ocean_state.reshape(cells * oy, columns)
    params = pltpu.CompilerParams(vmem_limit_bytes=32 * 1024 * 1024)
    near_out, far_out, ground = pl.pallas_call(
        functools.partial(edge_kernel, fields, levels, olev, oy),
        out_shape=(
            jax.ShapeDtypeStruct((HALO, columns), f32),
            jax.ShapeDtypeStruct((HALO, columns), f32),
            jax.ShapeDtypeStruct((fields * ay, columns), f32),
        ),
        in_specs=[pl.BlockSpec(memory_space=pltpu.HBM)] * 3,
        out_specs=(vmem, vmem, vmem),
        scratch_shapes=[
            pltpu.VMEM(atmos.shape, f32),
            pltpu.VMEM(ocean.shape, f32),
            pltpu.VMEM((EDGES, edge.shape[1]), jnp.bfloat16),
            pltpu.SemaphoreType.DMA((3,)),
        ],
        compiler_params=pltpu.CompilerParams(vmem_limit_bytes=ROOMLESS),
        name="edges",
    )(atmos, ocean, edge)
    far = lax.ppermute(far_out, "tile", pair_over(n))
    half = n // 2 * BLOCK
    kept, send = pl.pallas_call(
        functools.partial(share_kernel, n, fields),
        out_shape=(
            jax.ShapeDtypeStruct((n // 2 * (SLOTS + 1), GROUP, columns), f32),
            jax.ShapeDtypeStruct((n // 2 * (SLOTS + 1) + HALO // GROUP, GROUP, columns), f32),
        ),
        in_specs=[vmem] * 7,
        out_specs=(vmem, vmem),
        scratch_shapes=[
            pltpu.VMEM((ay, 8, columns), f32),
            pltpu.VMEM((n * (SLOTS + 1), GROUP, columns), f32),
            pltpu.SMEM((n,), jnp.int32),
        ],
        compiler_params=params,
        name="shares",
    )(*[a.reshape(1, -1) for a in (flux_coef, source_row, target_device, target_row)], ground, remap_weight, near_out)
    got = lax.ppermute(send.reshape(-1, columns), "tile", pair_up(n))
    near = got[half:]
    row_shape = jax.ShapeDtypeStruct((planes + cells, columns), f32)
    part_shapes = jax.ShapeDtypeStruct(atmos.shape, f32), jax.ShapeDtypeStruct(ocean.shape, f32)
    atmos_part, low, top, ocean_part = pl.pallas_call(
        functools.partial(inner_kernel, fields, levels, olev, oy),
        out_shape=(part_shapes[0], row_shape, row_shape, part_shapes[1]),
        in_specs=[vmem] * 3,
        out_specs=(vmem,) * 4,
        compiler_params=params,
        cost_estimate=cost(10**6),
        name="inner",
    )(atmos, ocean, mix)
    state = jnp.concatenate(
        [kept.reshape(n // 2, 1, BLOCK, columns), got[:half].reshape(n // 2, 1, BLOCK, columns)], axis=1
    )
    bit = 2
    while bit < n:
        pairs = state.reshape(state.shape[0] // 2, 2, state.shape[1], BLOCK, columns)
        keep, send = pairs[:, 0].reshape(-1, columns), pairs[:, 1].reshape(-1, columns)
        came = lax.ppermute(send, "tile", [(i, i ^ bit) for i in range(n)])
        if bit == 2:
            low, top, keep = pl.pallas_call(
                functools.partial(corner_kernel, planes),
                out_shape=(row_shape, row_shape, jax.ShapeDtypeStruct(keep.shape, f32)),
                in_specs=[vmem] * 6,
                out_specs=(vmem,) * 3,
                input_output_aliases={2: 0, 3: 1},
                compiler_params=params,
                cost_estimate=cost(10**9),
                name="corners",
            )(near, far, low, top, place, keep)
            up = lax.ppermute(low, "comp", [(i, (i + 1) % bands) for i in range(bands)])
            down = lax.ppermute(top, "comp", [(i, (i - 1) % bands) for i in range(bands)])
        state = jnp.concatenate(
            [keep.reshape(pairs[:, 0].shape), came.reshape(pairs[:, 0].shape)], axis=1
        )
        bit *= 2
    hbm = pl.BlockSpec(memory_space=pltpu.HBM)
    by_plane = jax.ShapeDtypeStruct((planes, ay, columns), f32)
    atmos_so_far, rims, ocean_part, remapped = pl.pallas_call(
        functools.partial(side_kernel, n, fields),
        out_shape=(
            by_plane,
            jax.ShapeDtypeStruct((2 * planes, columns), f32),
            part_shapes[1],
            jax.ShapeDtypeStruct((fields * oy, columns), f32),
        ),
        in_specs=[vmem] * 6,
        out_specs=(hbm, vmem, vmem, vmem),
        scratch_shapes=[
            pltpu.VMEM((ay - 2, planes, columns), f32),
            pltpu.SemaphoreType.DMA((ay - 2,)),
        ],
        compiler_params=params,
        cost_estimate=cost(10**8),
        name="sides",
    )(near, far, atmos_part, ocean_part, keep, place)
    atmos_next, ocean_next = pl.pallas_call(
        functools.partial(finish_kernel, bands, fields, levels),
        out_shape=(by_plane, jax.ShapeDtypeStruct((fields, olev * oy, columns), f32)),
        in_specs=[vmem] * 3 + [hbm] + [vmem] * 3,
        out_specs=(hbm, hbm),
        scratch_shapes=[
            pltpu.VMEM((2, planes, columns), f32),
            pltpu.VMEM((fields, olev * oy, columns), f32),
            pltpu.SemaphoreType.DMA((4,)),
        ],
        input_output_aliases={3: 0},
        compiler_params=params,
        name="finish",
    )(up, came, down, atmos_so_far, rims, ocean_part, remapped)
    return atmos_next.reshape(atmos_state.shape), ocean_next.reshape(ocean_state.shape)


def solution(mesh):
    return jax.shard_map(
        functools.partial(body, mesh),
        mesh=mesh,
        in_specs=(
            P(None, None, "comp", "tile"),
            P(None, None, "comp", "tile"),
            P(),
            P(("comp", "tile"), None, None),
            P(("comp", "tile")),
            P(("comp", "tile"), None),
            P(("comp", "tile")),
        ),
        out_specs=(P(None, None, "comp", "tile"), P(None, None, "comp", "tile")),
        check_vma=False,
    )
```

```python
import functools
import math

import jax
import jax.numpy as jnp
import numpy as np
from jax import lax
from jax.experimental import pallas as pl
from jax.experimental.pallas import tpu as pltpu
from jax.sharding import PartitionSpec as P

viscosity = 0.01
diffusion = 0.2
mixing_rate = 0.1
forcing_step = 0.5
SLOTS = 3
GROUP = 4
BLOCK = (SLOTS + 1) * GROUP
ROOMLESS = 55096 * 1024
EDGES = 32
HALO = 16


def gll_second():
    nodes = np.array([-1.0, -(0.2**0.5), 0.2**0.5, 1.0])
    derivative = np.zeros((4, 4))
    for i in range(4):
        for j in range(4):
            if i == j:
                derivative[i, j] = sum(1.0 / (nodes[i] - nodes[k]) for k in range(4) if k != i)
            else:
                top = np.prod([nodes[i] - nodes[k] for k in range(4) if k not in (i, j)])
                derivative[i, j] = top / np.prod([nodes[j] - nodes[k] for k in range(4) if k != j])
    return derivative @ derivative


def tables(columns):
    second = gll_second()
    along = np.kron(np.eye(columns // 4), second)
    seam = np.eye(columns)
    for x in range(0, columns, 4):
        for edge, other in ((x, x - 1), (x + 3, x + 4)):
            seam[edge, edge] = 0.5
            if 0 <= other < columns:
                seam[edge, other] = 0.5
    inner = (seam @ along).T
    first, last = np.eye(columns)[0], np.eye(columns)[-1]
    edge_atmos = np.zeros((16, 8 * columns))
    for k in range(8):
        for side, unit, row in ((0, first, along[0]), (8, last, along[-1])):
            edge_atmos[side + k, k * columns : (k + 1) * columns] += row
            for j in range(4):
                m = k // 4 * 4 + j
                edge_atmos[side + k, m * columns : (m + 1) * columns] += second[k % 4, j] * unit
    edge_ocean = np.zeros((8, 4 * columns))
    place_atmos = np.zeros((8, 16, columns))
    place_ocean = np.zeros((4, 16, columns))
    for c in range(4):
        edge_ocean[c, c * columns : (c + 1) * columns] = first
        edge_ocean[4 + c, c * columns : (c + 1) * columns] = last
        for part in (0, 8):
            place_ocean[c, part + c] = last
            place_ocean[c, part + 4 + c] = first
    for k in range(8):
        place_atmos[k, k] = 0.5 * first
        place_atmos[k, 8 + k] = 0.5 * last
    edge = np.zeros((128, 12 * columns))
    edge[:16, : 8 * columns] = edge_atmos
    edge[16:24, 8 * columns :] = edge_ocean
    bf = lambda a: jnp.asarray(a.astype(np.float32)).astype(jnp.bfloat16)
    return (
        bf(np.concatenate([inner, seam.T])),
        bf(edge),
        bf(np.concatenate([place_atmos.reshape(-1, columns), place_ocean.reshape(-1, columns)])),
    )


def dot(a, b):
    return jnp.dot(a, b, preferred_element_type=jnp.float32)


def dot_nt(a, b):
    return lax.dot_general(a, b, (((1,), (1,)), ((), ())), preferred_element_type=jnp.float32)


def dot_tn(a, b):
    return lax.dot_general(a, b, (((0,), (0,)), ((), ())), preferred_element_type=jnp.float32)


def split(v):
    high = v.astype(jnp.bfloat16)
    return high, (v - high.astype(jnp.float32)).astype(jnp.bfloat16)


def row_of(ref, k, count, stride):
    return ref[pl.ds(k, count, stride=stride), :]


def along_y(rows, k):
    second = gll_second()
    base = k // 4 * 4
    return sum(float(second[k % 4, j]) * rows[base + j] for j in range(4))


def edge_kernel(
    fields, levels, olev, oy, atmos_at, ocean_at, edge_at, near, far, ground, atmos, ocean, edge, sems
):
    planes, cells = fields * levels, fields * olev
    ay = atmos.shape[0] // planes
    columns = atmos.shape[1]
    copies = [
        pltpu.make_async_copy(atmos_at, atmos, sems.at[0]),
        pltpu.make_async_copy(edge_at.at[pl.ds(0, EDGES), :], edge, sems.at[1]),
        pltpu.make_async_copy(ocean_at, ocean, sems.at[2]),
    ]
    for copy in copies:
        copy.start()
    even = lax.axis_index("tile") % 2 == 0
    width = ay * columns
    copies[0].wait()
    copies[1].wait()
    halves = [row_of(atmos, k, planes, ay).astype(jnp.bfloat16) for k in range(ay)]
    cols = dot_nt(jnp.concatenate(halves, axis=1), edge[:, :width])
    for f in range(fields):
        ground[f * ay : (f + 1) * ay, :] = atmos[f * levels * ay : f * levels * ay + ay, :]
    copies[2].wait()
    cell_rows = [row_of(ocean, y, cells, oy) for y in range(oy)]
    chunks = [jnp.concatenate(cell_rows[4 * c : 4 * c + 4], axis=0) for c in range(oy // 4)]
    for part in zip(*[split(c) for c in chunks]):
        cols = cols + dot_nt(jnp.concatenate(part, axis=1), edge[:, width:])
    cols = cols.T
    atmos_cols, ocean_cols = cols[: 2 * ay], cols[2 * ay : 2 * ay + 8]
    left, right = atmos_cols[:ay], atmos_cols[ay:]
    near[:ay, :] = jnp.where(even, right, left)
    far[:ay, :] = jnp.where(even, left, right)
    near[ay:, :] = ocean_cols
    far[ay:, :] = ocean_cols


def swapped(offset):
    return (offset & ~6) | (offset & 2) << 1 | (offset & 4) >> 1


def share_kernel(
    n, fields, coef_in, source_in, target_in, target_row_in, ground, weight, near,
    keep, send, surf, blocks, counts,
):
    ay = ground.shape[0] // fields
    columns = ground.shape[1]
    items = weight.shape[0]
    half = n // 2 * (SLOTS + 1)
    me = lax.axis_index("tile")
    blocks[...] = jnp.full(blocks.shape, -1.0, jnp.float32)
    for y in range(ay):
        surf[y, fields:, :] = jnp.zeros((8 - fields, columns), jnp.float32)
    coef = coef_in[...]
    source, target, target_row = source_in[...], target_in[...], target_row_in[...]
    for f in range(fields):
        plane = ground[f * ay : (f + 1) * ay, :] * coef[0, f]
        for y in range(ay):
            surf[y, f : f + 1, :] = plane[y : y + 1]

    @pl.loop(0, n)
    def _(i):
        counts[i] = 0

    def some(first, many):
        results = [
            dot(surf[source[0, first + i]].astype(jnp.bfloat16), weight[first + i]) for i in range(many)
        ]
        for i in range(many):
            to = target[0, first + i]
            slot = counts[to]
            counts[to] = slot + 1
            offset = swapped(to ^ me)
            at = ((offset % 2) * (n // 2) + offset // 2) * (SLOTS + 1)
            blocks[at + slot] = results[i][:fields]
            blocks[at + SLOTS, pl.ds(slot, 1), :] = jnp.full(
                (1, columns), target_row[0, first + i].astype(jnp.float32)
            )

    many = math.gcd(items, 12)
    for part in range(items // many):
        some(part * many, many)
    keep[...] = blocks[:half]
    send[:half] = blocks[half:]
    for g in range(HALO // GROUP):
        send[half + g] = near[g * GROUP : (g + 1) * GROUP, :]


def inner_kernel(fields, levels, olev, oy, atmos, ocean, mix, atmos_part, low, top, ocean_part):
    planes, cells = fields * levels, fields * olev
    ay = atmos.shape[0] // planes
    columns = atmos.shape[1]
    rows = [row_of(atmos, k, planes, ay) for k in range(ay)]
    across = [
        dot(rows[k].astype(jnp.bfloat16), mix[:columns, :])
        + dot(along_y(rows, k).astype(jnp.bfloat16), mix[columns:, :])
        for k in range(ay)
    ]
    low[:planes, :] = across[ay - 1]
    top[:planes, :] = across[0]
    for k in range(ay):
        smooth = sum(share * across[j] for j, share in seam_rows(ay, k))
        atmos_part[k * planes : (k + 1) * planes, :] = rows[k] + viscosity * smooth
    col = lax.broadcasted_iota(jnp.int32, (cells, columns), 1)
    level = lax.broadcasted_iota(jnp.int32, (cells, columns), 0) % olev
    cell_rows = [row_of(ocean, y, cells, oy) for y in range(oy)]
    low[planes:, :] = cell_rows[oy - 1]
    top[planes:, :] = cell_rows[0]
    for y in range(oy):
        v = cell_rows[y]
        planar = (
            jnp.where(col == 0, 0.0, pltpu.roll(v, 1, 1))
            + jnp.where(col == columns - 1, 0.0, pltpu.roll(v, columns - 1, 1))
            - 4.0 * v
        )
        if y:
            planar = planar + cell_rows[y - 1]
        if y + 1 < oy:
            planar = planar + cell_rows[y + 1]
        upper = jnp.where(level == 0, v, pltpu.roll(v, 1, 0))
        lower = jnp.where(level == olev - 1, v, pltpu.roll(v, cells - 1, 0))
        vertical = upper + lower - 2.0 * v
        ocean_part[y * cells : (y + 1) * cells, :] = v + diffusion * planar + mixing_rate * vertical


def seam_rows(ay, k):
    if k % 4 == 0:
        return [(k, 0.5)] + ([(k - 1, 0.5)] if k else [])
    if k % 4 == 3:
        return [(k, 0.5)] + ([(k + 1, 0.5)] if k + 1 < ay else [])
    return [(k, 1.0)]


def corner_kernel(planes, near, far, low_in, top_in, place, later_in, low, top, later):
    ay = near.shape[0] - 8
    later[...] = later_in[...]
    halos = side_halos(lax.axis_index("tile") % 2 == 0, near[:ay, :], far[:ay, :])
    columns = place.shape[1]
    both = jnp.concatenate([place[(ay - 1) * 16 : ay * 16, :], place[:16, :]], axis=1)
    corners = dot_tn(halos, both)
    low[:planes, :] = low_in[:planes, :] + corners[:, :columns]
    top[:planes, :] = top_in[:planes, :] + corners[:, columns:]


def side_kernel(
    n, fields, near, far, atmos_in, ocean_in, blocks, place,
    atmos_out, rims, ocean_part, remapped, inside, sem,
):
    columns = near.shape[1]
    planes, ay = atmos_out.shape[:2]
    oy = remapped.shape[0] // fields
    cells = ocean_in.shape[0] // oy
    me = lax.axis_index("tile")
    even_tile = me % 2 == 0
    halos = side_halos(even_tile, near[:ay, :], far[:ay, :])
    sides = [dot_tn(halos, place[k * 16 : (k + 1) * 16, :]) for k in range(ay)]
    copies = []
    for k in range(ay):
        here = slice(k * planes, (k + 1) * planes)
        smooth = sum(share * sides[j] for j, share in seam_rows(ay, k))
        done = atmos_in[here, :] + viscosity * smooth
        if k in (0, ay - 1):
            rims[(planes if k else 0) : (2 * planes if k else planes), :] = done
        else:
            inside[k - 1] = done
            copies.append(pltpu.make_async_copy(inside.at[k - 1], atmos_out.at[:, k, :], sem.at[k - 1]))
            copies[-1].start()
    side = lax.broadcasted_iota(jnp.int32, (8, columns), 0)
    near_ocean, far_ocean = near[ay:, :], far[ay:, :]
    right_first = jnp.where(
        side < 4,
        jnp.where(me == n - 1, 0.0, jnp.where(even_tile, near_ocean, far_ocean)),
        jnp.where(me == 0, 0.0, jnp.where(even_tile, far_ocean, near_ocean)),
    )
    parts = jnp.concatenate(split(right_first), axis=0)
    for c in range(oy // 4):
        here = slice(c * 4 * cells, (c + 1) * 4 * cells)
        four = ocean_in[here, :] + diffusion * dot_tn(
            parts, place[(ay + c) * 16 : (ay + c + 1) * 16, :]
        )
        for j in range(4):
            ocean_part[pl.ds(4 * c + j, cells, stride=oy), :] = four[j * cells : (j + 1) * cells]
    remapped[...] = remap(blocks, fields, oy)
    for copy in copies:
        copy.wait()


def remap(blocks, fields, oy):
    rows, columns = blocks.shape
    lane = lax.broadcasted_iota(jnp.int32, (1, columns), 1)
    row_id = lax.broadcasted_iota(jnp.int32, (fields * oy, columns), 0)
    total = jnp.zeros((fields * oy, columns), jnp.float32)
    for start in range(0, rows, columns):
        count = min(columns, rows - start)
        ids = jnp.full((1, columns), -float(fields * oy), jnp.float32)
        for p in range(count // BLOCK):
            at = start + p * BLOCK + SLOTS * GROUP
            for slot in range(SLOTS):
                here = lane // GROUP == (p * BLOCK) // GROUP + slot
                ids = jnp.where(here, blocks[at + slot : at + slot + 1, :], ids)
        wanted = jnp.where(ids < 0, -1, ids.astype(jnp.int32) + lane % GROUP * oy)
        hitting = jnp.where(row_id == wanted, forcing_step, 0.0).astype(jnp.bfloat16)[:, :count]
        high, low = split(blocks[start : start + count, :])
        total = total + dot(hitting, high) + dot(hitting, low)
    return total


def side_halos(even_tile, near, far):
    left = jnp.where(even_tile, far, near)
    right = jnp.where(even_tile, near, far)
    return jnp.concatenate([left, right], axis=0).astype(jnp.bfloat16)


def finish_kernel(
    bands, fields, levels, up, came, down, atmos_so_far, rims, ocean_part, remapped,
    atmos_out, ocean_out, rims_out, cells_out, sems,
):
    planes = fields * levels
    ay = atmos_out.shape[1]
    cells = up.shape[0] - planes
    oy = ocean_part.shape[0] // cells
    olev = cells // fields
    band = lax.axis_index("comp")
    copies = []

    def send(src, dst):
        copies.append(pltpu.make_async_copy(src, dst, sems.at[len(copies)]))
        copies[-1].start()

    for slot, k, beyond in ((0, 0, up), (1, ay - 1, down)):
        rims_out[slot] = (
            rims[slot * planes : (slot + 1) * planes, :] + (0.5 * viscosity) * beyond[:planes, :]
        )
        send(rims_out.at[slot], atmos_out.at[:, k, :])
    for f in range(fields):
        cells_out[f] = ocean_part[f * olev * oy : (f + 1) * olev * oy, :]
    for y, beyond in (
        (0, jnp.where(band == 0, 0.0, up[planes:, :])),
        (oy - 1, jnp.where(band == bands - 1, 0.0, down[planes:, :])),
    ):
        row = pl.ds(y, olev, stride=oy)
        for f in range(fields):
            cells_out[f, row, :] = cells_out[f, row, :] + diffusion * beyond[f * olev : (f + 1) * olev]
    deep = pl.ds(oy, (olev - 1) * oy)
    send(cells_out.at[:, deep, :], ocean_out.at[:, deep, :])
    forcing = remapped[...] + remap(came, fields, oy)
    for f in range(fields):
        cells_out[f, :oy, :] = cells_out[f, :oy, :] + forcing[f * oy : (f + 1) * oy]
    top = pl.ds(0, oy)
    send(cells_out.at[:, top, :], ocean_out.at[:, top, :])
    for copy in copies:
        copy.wait()


def cost(flops):
    return pl.CostEstimate(flops=flops, bytes_accessed=10**6, transcendentals=0)


def pair_up(count):
    return [(i, i ^ 1) for i in range(count)]


def pair_over(count):
    return [(i, (i + 1) % count if i % 2 else (i - 1) % count) for i in range(count)]


def body(mesh, atmos_state, ocean_state, flux_coef, remap_weight, source_row, target_device, target_row):
    n, bands = mesh.shape["tile"], mesh.shape["comp"]
    fields, levels, ay, columns = atmos_state.shape
    olev, oy = ocean_state.shape[1:3]
    planes, cells = fields * levels, fields * olev
    f32 = jnp.float32
    vmem = pl.BlockSpec(memory_space=pltpu.VMEM)
    smem = pl.BlockSpec(memory_space=pltpu.SMEM)
    mix, edge, place = tables(columns)
    atmos = atmos_state.reshape(planes * ay, columns)
    ocean = ocean_state.reshape(cells * oy, columns)
    params = pltpu.CompilerParams(vmem_limit_bytes=32 * 1024 * 1024)
    near_out, far_out, ground = pl.pallas_call(
        functools.partial(edge_kernel, fields, levels, olev, oy),
        out_shape=(
            jax.ShapeDtypeStruct((HALO, columns), f32),
            jax.ShapeDtypeStruct((HALO, columns), f32),
            jax.ShapeDtypeStruct((fields * ay, columns), f32),
        ),
        in_specs=[pl.BlockSpec(memory_space=pltpu.HBM)] * 3,
        out_specs=(vmem, vmem, vmem),
        scratch_shapes=[
            pltpu.VMEM(atmos.shape, f32),
            pltpu.VMEM(ocean.shape, f32),
            pltpu.VMEM((EDGES, edge.shape[1]), jnp.bfloat16),
            pltpu.SemaphoreType.DMA((3,)),
        ],
        compiler_params=pltpu.CompilerParams(vmem_limit_bytes=ROOMLESS),
        name="edges",
    )(atmos, ocean, edge)
    far = lax.ppermute(far_out, "tile", pair_over(n))
    half = n // 2 * BLOCK
    kept, send = pl.pallas_call(
        functools.partial(share_kernel, n, fields),
        out_shape=(
            jax.ShapeDtypeStruct((n // 2 * (SLOTS + 1), GROUP, columns), f32),
            jax.ShapeDtypeStruct((n // 2 * (SLOTS + 1) + HALO // GROUP, GROUP, columns), f32),
        ),
        in_specs=[vmem] * 7,
        out_specs=(vmem, vmem),
        scratch_shapes=[
            pltpu.VMEM((ay, 8, columns), f32),
            pltpu.VMEM((n * (SLOTS + 1), GROUP, columns), f32),
            pltpu.SMEM((n,), jnp.int32),
        ],
        compiler_params=params,
        name="shares",
    )(*[a.reshape(1, -1) for a in (flux_coef, source_row, target_device, target_row)], ground, remap_weight, near_out)
    got = lax.ppermute(send.reshape(-1, columns), "tile", pair_up(n))
    near = got[half:]
    row_shape = jax.ShapeDtypeStruct((planes + cells, columns), f32)
    part_shapes = jax.ShapeDtypeStruct(atmos.shape, f32), jax.ShapeDtypeStruct(ocean.shape, f32)
    atmos_part, low, top, ocean_part = pl.pallas_call(
        functools.partial(inner_kernel, fields, levels, olev, oy),
        out_shape=(part_shapes[0], row_shape, row_shape, part_shapes[1]),
        in_specs=[vmem] * 3,
        out_specs=(vmem,) * 4,
        compiler_params=params,
        cost_estimate=cost(10**6),
        name="inner",
    )(atmos, ocean, mix)
    state = jnp.concatenate(
        [kept.reshape(n // 2, 1, BLOCK, columns), got[:half].reshape(n // 2, 1, BLOCK, columns)], axis=1
    )
    bit = 2
    while bit < n:
        pairs = state.reshape(state.shape[0] // 2, 2, state.shape[1], BLOCK, columns)
        keep, send = pairs[:, 0].reshape(-1, columns), pairs[:, 1].reshape(-1, columns)
        came = lax.ppermute(send, "tile", [(i, i ^ swapped(bit)) for i in range(n)])
        if bit == 2:
            low, top, keep = pl.pallas_call(
                functools.partial(corner_kernel, planes),
                out_shape=(row_shape, row_shape, jax.ShapeDtypeStruct(keep.shape, f32)),
                in_specs=[vmem] * 6,
                out_specs=(vmem,) * 3,
                input_output_aliases={2: 0, 3: 1},
                compiler_params=params,
                cost_estimate=cost(10**9),
                name="corners",
            )(near, far, low, top, place, keep)
            up = lax.ppermute(low, "comp", [(i, (i + 1) % bands) for i in range(bands)])
            down = lax.ppermute(top, "comp", [(i, (i - 1) % bands) for i in range(bands)])
        state = jnp.concatenate(
            [keep.reshape(pairs[:, 0].shape), came.reshape(pairs[:, 0].shape)], axis=1
        )
        bit *= 2
    hbm = pl.BlockSpec(memory_space=pltpu.HBM)
    by_plane = jax.ShapeDtypeStruct((planes, ay, columns), f32)
    atmos_so_far, rims, ocean_part, remapped = pl.pallas_call(
        functools.partial(side_kernel, n, fields),
        out_shape=(
            by_plane,
            jax.ShapeDtypeStruct((2 * planes, columns), f32),
            part_shapes[1],
            jax.ShapeDtypeStruct((fields * oy, columns), f32),
        ),
        in_specs=[vmem] * 6,
        out_specs=(hbm, vmem, vmem, vmem),
        scratch_shapes=[
            pltpu.VMEM((ay - 2, planes, columns), f32),
            pltpu.SemaphoreType.DMA((ay - 2,)),
        ],
        compiler_params=params,
        cost_estimate=cost(10**8),
        name="sides",
    )(near, far, atmos_part, ocean_part, keep, place)
    atmos_next, ocean_next = pl.pallas_call(
        functools.partial(finish_kernel, bands, fields, levels),
        out_shape=(by_plane, jax.ShapeDtypeStruct((fields, olev * oy, columns), f32)),
        in_specs=[vmem] * 3 + [hbm] + [vmem] * 3,
        out_specs=(hbm, hbm),
        scratch_shapes=[
            pltpu.VMEM((2, planes, columns), f32),
            pltpu.VMEM((fields, olev * oy, columns), f32),
            pltpu.SemaphoreType.DMA((4,)),
        ],
        input_output_aliases={3: 0},
        compiler_params=params,
        name="finish",
    )(up, came, down, atmos_so_far, rims, ocean_part, remapped)
    return atmos_next.reshape(atmos_state.shape), ocean_next.reshape(ocean_state.shape)


def solution(mesh):
    return jax.shard_map(
        functools.partial(body, mesh),
        mesh=mesh,
        in_specs=(
            P(None, None, "comp", "tile"),
            P(None, None, "comp", "tile"),
            P(),
            P(("comp", "tile"), None, None),
            P(("comp", "tile")),
            P(("comp", "tile"), None),
            P(("comp", "tile")),
        ),
        out_specs=(P(None, None, "comp", "tile"), P(None, None, "comp", "tile")),
        check_vma=False,
    )
```
